128 devices in a mesh: azim: 32 (over x, y, core), axial: 4 (over z).
Axes of the slice: x: 4, y: 4, z: 4, core: 2. Of those that a mesh axis runs over, the one named last changes fastest.
Arguments:
- fluid_vel: float32 [3, 128, 64, 128], P(None, 'azim', 'axial'), may hold values from -6 to 6
- pressure: float32 [128, 64, 128], P('azim', 'axial'), may hold values from -6 to 6
- part_vel: float32 [65536, 3, 128], P(('azim', 'axial')), may hold values from -6 to 6
- part_vol: float32 [65536, 128], P(('azim', 'axial')), may hold values from 0.05 to 0.5
- part_drag: float32 [65536, 128], P(('azim', 'axial')), may hold values from 0.5 to 4
- cell_of: int32 [65536, 128], P(('azim', 'axial')), may hold values from 0 to 8191
- dest_of: int32 [65536, 1], P(('azim', 'axial')), may hold values from 0 to 31; in each aligned block of 512 rows (0 to 511, 512 to 1023, ...) at most 32 rows name the same one
Outputs:
- fluid_out: float32 [3, 128, 64, 128], P(None, 'azim', 'axial')
- part_out: float32 [65536, 3, 128], P(('azim', 'axial'))
The draws below stay inside these ranges and needn't reach their ends.
Inputs may be any that keep to these rules, and one draw needn't show every extreme that they name: `dest_of`: among the 512 blocks of one device, at most 32 name the same owner, and in every draw some owner is named by exactly 32 of them.
All inputs are finite; a program needn't handle non-finite values.
Results may differ from the reference program's by a relative error of at most 0.00007.
Values sent between devices are 32-bit elements; how exact they have to be, the bound alone decides.
No kernel may reach another device: no remote copies, remote signals or barrier semaphores. Data moves between devices by JAX's collectives and lax.ppermute only.
A program may use at most 64 MiB of HBM per device.

```python
import math
import jax
import jax.numpy as jnp
import numpy as np

CA = 4
CZ = 16
R = 128
NB = 512
PB = 128
CAP = 32
NA = 128
NZ = 64
CELLS = 8192
BLOCKS = 65536
N_AZIM = 32
N_AXIAL = 4


def plant(array, own_key, low, high):
    longest = array.shape.index(max(array.shape))
    spots = []
    for shift in (0, 1):
        where = [jax.random.randint(jax.random.fold_in(own_key, axis), (), 0, length) for axis, length in enumerate(array.shape)]
        where[longest] = (where[longest] + shift) % array.shape[longest]
        spots.append(tuple(where))
    return array.at[spots[0]].set(low).at[spots[1]].set(high)


def block_levels(own_key, shape, pieces, smallest, high):
    gain = 1.0
    for position, blocks in pieces:
        heights = jax.random.uniform(jax.random.fold_in(jax.random.fold_in(own_key, 6), position), (blocks,), jnp.float32, smallest / len(pieces), high / len(pieces))
        gain = gain * jnp.repeat(jnp.exp(heights), shape[position] // blocks).reshape((-1,) + (1,) * (len(shape) - 1 - position))
    return gain


def deal_out(stream_key, own, number, rows, number_of, top, limit, skew):
    sequence = jax.random.permutation(stream_key, number_of)
    heavy_load, ordinary = portions_of(number_of, rows * top, limit, skew, True), portions_of(number_of, rows * top, limit, skew, False)
    places = jnp.arange(number_of)

    def named(tallies, offset_by):
        used = int((tallies > 0).sum())
        fixed = max(1, used // 4)
        shifted = fixed + (places - fixed + offset_by * (used - fixed)) % max(1, number_of - fixed)
        return jnp.zeros((number_of,), jnp.int32).at[sequence[jnp.where(places < fixed, places, shifted)]].set(jnp.asarray(tallies, jnp.int32))

    tallies = jnp.where(number % 4 == 0, named(heavy_load, number // 4), named(ordinary, number - number // 4 - 1))
    mixed = jax.random.permutation(jax.random.fold_in(own, 3), number_of)
    source_of, taker = mixed[0:number_of // 2 * 2:2], mixed[1:number_of // 2 * 2:2]
    slack = jnp.minimum(tallies[source_of] - 1, limit - tallies[taker]) // 2
    slack = jnp.where((source_of == sequence[0]) | (taker == sequence[0]) | (tallies[taker] == 0), 0, jnp.maximum(slack, 0))
    shifted = jax.random.randint(jax.random.fold_in(own, 4), (number_of // 2,), 0, 1 << 20) % (slack + 1)
    tallies = tallies.at[source_of].add(-shifted).at[taker].add(shifted)
    labels = jnp.searchsorted(jnp.cumsum(tallies), jnp.arange(rows * top), side="right").astype(jnp.int32)
    table = labels.reshape(top, rows).T
    table = table[jax.random.permutation(jax.random.fold_in(own, 1), rows)]
    offset_by = jax.random.randint(jax.random.fold_in(own, 2), (rows, 1), 0, top)
    return jnp.take_along_axis(table, (jnp.arange(top)[None, :] + offset_by) % top, axis=1)


def portions_of(count, total, most, skew, full):
    portions = [(1 << 20) // math.isqrt(rank ** skew) + 1 for rank in range(1, count + 1)]
    largest = most if full else min(most, max(-(-total // count), total * portions[0] // sum(portions)))
    least = 1 if total - largest >= count - 1 else 0
    holding, rest = [largest] + [least] * (count - 1), total - largest - least * (count - 1)
    while rest > 0:
        candidates = [i for i in range(1, count) if holding[i] < largest] or [i for i in range(1, count) if holding[i] < most]
        pool, left = sum([portions[i] for i in candidates]), rest
        for i in candidates:
            extra = min(most - holding[i], max(1, left * portions[i] // pool), rest)
            holding[i] = holding[i] + extra
            rest = rest - extra
    return np.array(holding)


def scatter_about(rng, shape, scale, reach, shards=(), kind=jnp.bfloat16):
    factor_of = block_levels(rng, shape, shards, -0.22, 0.18) if shards else 1.0
    entries = jax.random.normal(rng, shape, jnp.float32) * scale * factor_of
    return jnp.minimum(jnp.maximum(entries, -reach), reach).astype(kind)


def setup_inputs(seed: int = 0) -> dict:
    keys = jax.random.split(jax.random.key(seed), 8)
    fluid_vel = scatter_about(keys[0], (3, NA, NZ, R), 1.0, 6.0, ((1, 32), (2, 4)), jnp.float32)
    pressure = scatter_about(keys[1], (NA, NZ, R), 1.0, 6.0, ((0, 32), (1, 4)), jnp.float32)
    part_vel = scatter_about(keys[2], (BLOCKS, 3, PB), 1.0, 6.0, ((0, 128),), jnp.float32)
    part_vol = jnp.clip(jnp.exp(math.log(0.5) - 2.3025851 * jax.random.uniform(keys[3], (BLOCKS, PB), jnp.float32) ** block_levels(keys[3], (BLOCKS, PB), ((0, 128),), -0.2, 0.2)), 0.05, 0.5)
    part_drag = jnp.clip(jnp.exp(math.log(4.0) - 2.0794415 * jax.random.uniform(keys[4], (BLOCKS, PB), jnp.float32) ** block_levels(keys[4], (BLOCKS, PB), ((0, 128),), -0.2, 0.2)), 0.5, 4.0)
    cell_of = plant(jax.random.randint(keys[5], (BLOCKS, PB), 0, CELLS), jax.random.fold_in(keys[5], 1), 0, CELLS - 1).astype(jnp.int32)
    dest_of_keys = jax.random.split(jax.random.fold_in(keys[6], 1), BLOCKS // NB)
    dest_of_turns = jax.random.permutation(jax.random.fold_in(keys[6], 3), BLOCKS // NB)
    dest_of = jax.vmap(lambda own, number: deal_out(jax.random.fold_in(keys[6], 2), own, number, NB, N_AZIM, 1, CAP, 2))(dest_of_keys, dest_of_turns).reshape((BLOCKS, 1))
    return {"fluid_vel": fluid_vel, "pressure": pressure, "part_vel": part_vel, "part_vol": part_vol, "part_drag": part_drag, "cell_of": cell_of, "dest_of": dest_of}


TIME_STEP = 0.25
VISCOSITY = 0.5


def combine(stacked, solid, source, neighbours):
    padded = jnp.pad(stacked, ((0, 0), (0, 0), (0, 0), (1, 1)))
    every = neighbours + [padded[..., 2:], padded[..., :-2]]
    voidage = stacked[0]
    flow = stacked[2:]
    spread = jnp.zeros_like(flow)
    for other in every:
        spread = spread + 0.5 * (voidage + other[0]) * (other[2:] - flow)
    slope = 0.5 * jnp.stack([every[0][1] - every[1][1], every[2][1] - every[3][1], every[4][1] - every[5][1]])
    return flow + TIME_STEP * ((1.0 + solid) * (VISCOSITY * spread + source) - slope)


def reference(fluid_vel, pressure, part_vel, part_vol, part_drag, cell_of, dest_of):
    blocks = part_vol.shape[0]
    device_ids = jnp.arange(blocks, dtype=jnp.int32) // NB
    axial_ids = device_ids % N_AXIAL
    destination = dest_of[:, 0]
    tile_row = cell_of // R
    tile_col = cell_of % R
    glob_azim = destination[:, None] * CA + tile_row // CZ
    glob_axial = axial_ids[:, None] * CZ + tile_row % CZ
    flat_cell = ((glob_azim * NZ + glob_axial) * R + tile_col).reshape(-1).astype(jnp.int32)
    cell_count = NA * NZ * R
    volume = part_vol.reshape(-1)
    solid = jax.ops.segment_sum(volume, flat_cell, num_segments=cell_count)
    flow_flat = fluid_vel.reshape(3, cell_count)
    flow_here = flow_flat[:, flat_cell]
    solid_here = solid[flat_cell]
    velocity = jnp.transpose(part_vel, (1, 0, 2)).reshape(3, -1)
    drag_rate = part_drag.reshape(-1) * (1.0 + solid_here)
    new_vel = (velocity + TIME_STEP * drag_rate * flow_here) / (1.0 + TIME_STEP * drag_rate)
    push_force = volume * drag_rate * (new_vel - flow_here)
    source = jax.vmap(lambda column: jax.ops.segment_sum(column, flat_cell, num_segments=cell_count))(push_force)
    source = source.reshape(3, NA, NZ, R)
    solid = solid.reshape(NA, NZ, R)
    voidage = 1.0 / (1.0 + solid)
    stacked = jnp.concatenate([voidage[None], pressure[None], fluid_vel], 0)
    padded = jnp.pad(stacked, ((0, 0), (0, 0), (1, 1), (0, 0)))
    neighbours = [jnp.roll(stacked, -1, axis=1), jnp.roll(stacked, 1, axis=1), padded[:, :, 2:], padded[:, :, :-2]]
    fluid_out = combine(stacked, solid, source, neighbours)
    part_out = jnp.transpose(new_vel.reshape(3, blocks, PB), (1, 0, 2))
    return fluid_out, part_out
```

```python
import functools

import jax
import jax.numpy as jnp
from jax import lax
from jax.experimental import pallas as pl
from jax.experimental.pallas import tpu as pltpu
from jax.sharding import PartitionSpec as P

TIME_STEP = 0.25
VISCOSITY = 0.5
BF, F32, I32 = jnp.bfloat16, jnp.float32, jnp.int32
LANES = 128
HALF = 32
VMEM_LIMIT = 60 * 2**20


def row(ref, b):
    return ref[pl.ds(b, 1), :]


def two_parts(value):
    high = value.astype(BF)
    return high, (value - high.astype(F32)).astype(BF)


def columns_of(cell):
    return (cell & 127) | ((cell >> 12) << 7)


def scatter_rows(dest_ref, cell_ref, value_of, fields, out_ref, turned_ref, unroll):
    blocks = cell_ref.shape[0]
    groups = blocks // LANES
    out_ref[...] = jnp.zeros_like(out_ref)
    for g in range(groups):
        ids = columns_of(cell_ref[g * LANES : (g + 1) * LANES, :])
        turned_ref[g] = ids.astype(F32).T.astype(BF)
    lane = lax.broadcasted_iota(I32, (LANES, LANES), 1)
    lanes = [(lane + k * LANES).astype(F32).astype(BF) for k in range(2)]
    rows = lax.broadcasted_iota(I32, (HALF, LANES), 0).astype(F32).astype(BF)
    one, zero = jnp.ones((), BF), jnp.zeros((), BF)

    def product(g, j):
        b = g * LANES + j
        in_half = ((row(cell_ref, b) >> 7) & (HALF - 1)).astype(F32).astype(BF)
        mask = rows == jnp.broadcast_to(in_half, (HALF, LANES))
        parts = []
        for f in range(fields):
            high, low = two_parts(value_of(f, b))
            parts.append(jnp.where(mask, jnp.broadcast_to(high, (HALF, LANES)), zero))
            parts.append(jnp.where(mask, jnp.broadcast_to(low, (HALF, LANES)), zero))
        spread = jnp.broadcast_to(turned_ref[g][:, j : j + 1], (LANES, LANES))
        hot = jnp.concatenate([jnp.where(k == spread, one, zero) for k in lanes], axis=1)
        return jnp.dot(jnp.concatenate(parts, axis=0), hot, preferred_element_type=F32)

    def step(g, carry):
        for i in range(LANES // unroll):
            first = i * unroll
            got = [(first + u, product(g, first + u)) for u in range(unroll)]
            for j, res in got:
                d = dest_ref[g * LANES + j]
                for f in range(fields):
                    at = 2 * f * HALF
                    both = res[at : at + HALF] + res[at + HALF : at + 2 * HALF]
                    out_ref[d, f, 0:HALF, :] += both[:, :LANES]
                    out_ref[d, f, HALF : 2 * HALF, :] += both[:, LANES:]
        return carry

    lax.fori_loop(0, groups, step, 0)


def deposit_kernel(dest_ref, cell_ref, vol_ref, out_ref, turned_ref):
    scatter_rows(dest_ref, cell_ref, lambda f, b: row(vol_ref, b), 1, out_ref, turned_ref, 16)


def source_kernel(dest_ref, cell_ref, push_ref, out_ref, turned_ref):
    scatter_rows(
        dest_ref, cell_ref, lambda f, b: push_ref[f, pl.ds(b, 1), :], 3, out_ref, turned_ref, 8
    )


SMEM_SPEC = pl.BlockSpec(memory_space=pltpu.SMEM)
VMEM_SPEC = pl.BlockSpec(memory_space=pltpu.VMEM)
ANY_SPEC = pl.BlockSpec(memory_space=pl.ANY)


def scatter(kernel, dest, cell, values, fields, tiles, tile_rows):
    blocks = cell.shape[0]
    return pl.pallas_call(
        kernel,
        out_shape=jax.ShapeDtypeStruct((tiles, fields, tile_rows, LANES), F32),
        in_specs=[SMEM_SPEC, VMEM_SPEC, VMEM_SPEC],
        out_specs=VMEM_SPEC,
        scratch_shapes=[pltpu.VMEM((blocks // LANES, LANES, LANES), BF)],
        compiler_params=pltpu.CompilerParams(vmem_limit_bytes=VMEM_LIMIT),
    )(dest, cell, values)


def pick_rows(dest_ref, cell_ref, table_ref, fields, store, unroll):
    blocks = cell_ref.shape[0]
    eights = table_ref.shape[2] // 8
    sub = lax.broadcasted_iota(I32, (8, LANES), 0)

    def step(i, carry):
        for u in range(unroll):
            b = i * unroll + u
            d = dest_ref[b]
            cell = jnp.broadcast_to(row(cell_ref, b), (8, LANES))
            column = cell & 127
            top = cell >> 10
            low = (cell >> 7) & 7
            for f in range(fields):
                acc = None
                for q in range(eights):
                    got = jnp.take_along_axis(
                        table_ref[d, f, 8 * q : 8 * q + 8, :],
                        column,
                        axis=1,
                        mode="promise_in_bounds",
                    )
                    acc = got if acc is None else jnp.where(top == q, got, acc)
                store(f, b, jnp.sum(jnp.where(sub == low, acc, 0.0), axis=0, keepdims=True))
        return carry

    lax.fori_loop(0, blocks // unroll, step, 0)


def load_tables(same_ref, other_ref, table_ref, sems):
    near = same_ref.shape[0]
    copies = [
        pltpu.make_async_copy(same_ref, table_ref.at[pl.ds(0, near)], sems.at[0]),
        pltpu.make_async_copy(other_ref, table_ref.at[pl.ds(near, near)], sems.at[1]),
    ]
    for copy in copies:
        copy.start()
    for copy in copies:
        copy.wait()


def flow_kernel(dest_ref, cell_ref, same_ref, other_ref, out_ref, table_ref, sems):
    load_tables(same_ref, other_ref, table_ref, sems)

    def store(f, b, value):
        out_ref[f, pl.ds(b, 1), :] = value

    pick_rows(dest_ref, cell_ref, table_ref, 3, store, 16)


def particle_kernel(
    dest_ref, cell_ref, vol_ref, drag_ref, vel_ref, flow_ref, same_ref, other_ref,
    new_ref, push_ref, table_ref, solid_ref, sems,
):
    load_tables(same_ref, other_ref, table_ref, sems)

    def store(f, b, value):
        solid_ref[pl.ds(b, 1), :] = value

    pick_rows(dest_ref, cell_ref, table_ref, 1, store, 16)
    blocks = cell_ref.shape[0]
    chunk = 32

    def step(i, carry):
        at = pl.ds(pl.multiple_of(i * chunk, chunk), chunk)
        rate = drag_ref[at, :] * (1.0 + solid_ref[at, :])
        weight = vol_ref[at, :] * rate
        scaled = TIME_STEP * rate
        below = 1.0 / (1.0 + scaled)
        for f in range(3):
            here = flow_ref[f, at, :]
            new = (vel_ref[f, at, :] + scaled * here) * below
            new_ref[f, at, :] = new
            push_ref[f, at, :] = weight * (new - here)
        return carry

    lax.fori_loop(0, blocks // chunk, step, 0, unroll=2)


def combine(stacked, solid, source, neighbours):
    padded = jnp.pad(stacked, ((0, 0), (0, 0), (0, 0), (1, 1)))
    every = neighbours + [padded[..., 2:], padded[..., :-2]]
    voidage = stacked[0]
    flow = stacked[2:]
    spread = jnp.zeros_like(flow)
    for other in every:
        spread = spread + 0.5 * (voidage + other[0]) * (other[2:] - flow)
    slope = 0.5 * jnp.stack(
        [every[0][1] - every[1][1], every[2][1] - every[3][1], every[4][1] - every[5][1]]
    )
    return flow + TIME_STEP * ((1.0 + solid) * (VISCOSITY * spread + source) - slope)


def padded_2(value, sides, width, wrap):
    for axis, dim in sides:
        size, length = (lax.axis_size(axis), value.shape[dim])
        up = [(i, (i + 1) % size) for i in range(size if wrap else size - 1)]
        down = [(j, i) for i, j in up]
        last = lax.slice_in_dim(value, length - width, length, axis=dim)
        first = lax.slice_in_dim(value, 0, width, axis=dim)
        before = lax.ppermute(last, axis, up)
        after = lax.ppermute(first, axis, down)
        value = jnp.concatenate([before, value, after], axis=dim)
    return value


def on_device(fluid_vel, pressure, part_vel, part_vol, part_drag, cell_of, dest_of):
    size = lax.axis_size("azim")
    near = size // 2
    blocks, block_rows = part_vol.shape
    tile_azim, tile_axial, radial = pressure.shape
    tile_rows = tile_azim * tile_axial
    core = lax.axis_index("azim") % 2
    chips = [[2 * i + c for i in range(near)] for c in range(2)]
    twin = [(i, i ^ 1) for i in range(size)]
    dest = dest_of[:, 0]
    slot = ((dest & 1) ^ core) * near + (dest >> 1)

    def exchange(value):
        return lax.all_to_all(
            value, "azim", split_axis=0, concat_axis=0, tiled=True, axis_index_groups=chips
        )

    def summed(parts):
        other = lax.ppermute(parts[near:], "azim", twin)
        got = exchange(parts[:near] + other)
        return jnp.sum(got, axis=0)

    def gathered(tile):
        same = exchange(jnp.broadcast_to(tile[None], (near,) + tile.shape))
        return same, lax.ppermute(same, "azim", twin)

    flow_tile = fluid_vel.reshape(3, tile_rows, radial)
    flow_same, flow_other = gathered(flow_tile)
    solid_parts = scatter(deposit_kernel, slot, cell_of, part_vol, 1, size, tile_rows)
    solid_flat = summed(solid_parts)
    solid_same, solid_other = gathered(solid_flat)
    params = pltpu.CompilerParams(vmem_limit_bytes=VMEM_LIMIT)
    per_particle = jax.ShapeDtypeStruct((3, blocks, block_rows), F32)
    flow_here = pl.pallas_call(
        flow_kernel,
        out_shape=per_particle,
        in_specs=[SMEM_SPEC, VMEM_SPEC, ANY_SPEC, ANY_SPEC],
        out_specs=VMEM_SPEC,
        scratch_shapes=[
            pltpu.VMEM((size, 3, tile_rows, radial), F32),
            pltpu.SemaphoreType.DMA((2,)),
        ],
        compiler_params=params,
    )(slot, cell_of, flow_same, flow_other)
    new_vel, push = pl.pallas_call(
        particle_kernel,
        out_shape=(per_particle, per_particle),
        in_specs=[SMEM_SPEC] + [VMEM_SPEC] * 5 + [ANY_SPEC] * 2,
        out_specs=(VMEM_SPEC, VMEM_SPEC),
        scratch_shapes=[
            pltpu.VMEM((size, 1, tile_rows, radial), F32),
            pltpu.VMEM((blocks, block_rows), F32),
            pltpu.SemaphoreType.DMA((2,)),
        ],
        compiler_params=params,
    )(
        slot, cell_of, part_vol, part_drag, jnp.transpose(part_vel, (1, 0, 2)), flow_here,
        solid_same, solid_other,
    )
    source_parts = scatter(source_kernel, slot, cell_of, push, 3, size, tile_rows)
    source_flat = summed(source_parts)
    part_out = jnp.transpose(new_vel, (1, 0, 2))
    solid = solid_flat.reshape(tile_azim, tile_axial, radial)
    source = source_flat.reshape(3, tile_azim, tile_axial, radial)
    voidage = 1.0 / (1.0 + solid)
    stacked = jnp.concatenate([voidage[None], pressure[None], fluid_vel], 0)
    cycle_fields = padded_2(stacked, (("azim", 1),), 1, True)
    axial_fields = padded_2(stacked, (("axial", 2),), 1, False)
    neighbours = [
        cycle_fields[:, 2:],
        cycle_fields[:, :-2],
        axial_fields[:, :, 2:],
        axial_fields[:, :, :-2],
    ]
    fluid_out = combine(stacked, solid, source, neighbours)
    return (fluid_out, part_out)


def solution(mesh):
    in_specs = (
        P(None, "azim", "axial", None),
        P("azim", "axial", None),
        P(("azim", "axial"), None, None),
        P(("azim", "axial"), None),
        P(("azim", "axial"), None),
        P(("azim", "axial"), None),
        P(("azim", "axial"), None),
    )
    out_specs = (P(None, "azim", "axial", None), P(("azim", "axial"), None, None))
    return jax.shard_map(
        on_device, mesh=mesh, in_specs=in_specs, out_specs=out_specs, check_vma=False
    )
```

```python
import functools

import jax
import jax.numpy as jnp
from jax import lax
from jax.experimental import pallas as pl
from jax.experimental.pallas import tpu as pltpu
from jax.sharding import PartitionSpec as P

TIME_STEP = 0.25
VISCOSITY = 0.5
BF, F32, I32, I16 = jnp.bfloat16, jnp.float32, jnp.int32, jnp.int16
LANES = 128
HALF = 32
CHUNKS = 4
SIDE = 4
SMEM_SPEC = pl.BlockSpec(memory_space=pltpu.SMEM)
VMEM_SPEC = pl.BlockSpec(memory_space=pltpu.VMEM)
ANY_SPEC = pl.BlockSpec(memory_space=pl.ANY)
PARAMS = pltpu.CompilerParams(vmem_limit_bytes=60 * 2**20)


def cost(micros):
    return pl.CostEstimate(flops=0, transcendentals=0, bytes_accessed=int(micros * 3_000_000))


def row(ref, b):
    return ref[pl.ds(b, 1), :]


def two_parts(value):
    high = value.astype(BF)
    return high, (value - high.astype(F32)).astype(BF)


def columns_of(cell):
    return (cell & 127) | ((cell >> 12) << 7)


def ramps():
    lane = lax.broadcasted_iota(I32, (LANES, LANES), 1)
    lanes = [(lane + k * LANES).astype(I16) for k in range(2)]
    rows = lax.broadcasted_iota(I32, (HALF, LANES), 0).astype(F32).astype(BF)
    return lanes, rows


def weighted_rows(cell, values, rows):
    in_half = jnp.where(cell < 0, -1, (cell >> 7) & (HALF - 1)).astype(F32).astype(BF)
    mask = rows == jnp.broadcast_to(in_half, (HALF, LANES))
    zero = jnp.zeros((), BF)
    parts = []
    for value in values:
        for part in two_parts(value):
            parts.append(jnp.where(mask, jnp.broadcast_to(part, (HALF, LANES)), zero))
    return jnp.concatenate(parts, axis=0)


def hot_columns(words, j, lanes):
    one, zero = jnp.ones((), BF), jnp.zeros((), BF)
    word = jnp.broadcast_to(words[:, j : j + 1], (LANES, LANES)).astype(I16)
    both = (word & 255, lax.shift_right_logical(word, jnp.int16(8)))
    return [
        jnp.concatenate([jnp.where(k == ids, one, zero) for k in lanes], axis=1) for ids in both
    ]


def add_to(sum_ref, d, res, fields):
    for f in range(fields):
        at = 2 * f * HALF
        both = res[at : at + HALF] + res[at + HALF : at + 2 * HALF]
        sum_ref[d, f, 0:HALF, :] += both[:, :LANES]
        sum_ref[d, f, HALF : 2 * HALF, :] += both[:, LANES:]


def start_all(pairs, sems):
    copies = [pltpu.make_async_copy(a, b, sems.at[i]) for i, (a, b) in enumerate(pairs)]
    for copy in copies:
        copy.start()
    return copies


def wait_all(copies):
    for copy in copies:
        copy.wait()


def halves(ref):
    near = ref.shape[0] // 2
    return ref.at[pl.ds(0, near)], ref.at[pl.ds(near, near)]


def deposit_kernel(
    slot_ref, cell_ref, vol_ref, tile_ref, same_ref, other_ref, late_ref, sum_ref, words_ref, sems
):
    late_ref[...] = tile_ref[...]
    sum_ref[...] = jnp.zeros_like(sum_ref)
    blocks = cell_ref.shape[0]
    for g in range(blocks // 256):
        a = columns_of(cell_ref[g * 256 : g * 256 + 128, :])
        b = columns_of(cell_ref[g * 256 + 128 : g * 256 + 256, :])
        words_ref[g] = (a | (b << 8)).astype(F32).T.astype(I32)
    lanes, rows = ramps()
    unroll = 8

    def step(g, carry):
        for i in range(LANES // unroll):
            got = []
            for u in range(unroll):
                j = i * unroll + u
                hots = hot_columns(words_ref[g], j, lanes)
                for s in range(2):
                    b = g * 256 + s * 128 + j
                    left = weighted_rows(row(cell_ref, b), [row(vol_ref, b)], rows)
                    got.append((b, jnp.dot(left, hots[s], preferred_element_type=F32)))
            for b, res in got:
                add_to(sum_ref, slot_ref[b], res, 1)
        return carry

    lax.fori_loop(0, blocks // 256, step, 0)
    low, high = halves(sum_ref)
    out = [
        pltpu.make_async_copy(high, other_ref, sems.at[0]),
        pltpu.make_async_copy(low, same_ref, sems.at[1]),
    ]
    for copy in out:
        copy.start()
    wait_all(out)


def join_kernel(same_ref, other_ref, *refs):
    tile_refs, (parts_ref, tiles_ref) = refs[:-2], refs[-2:]
    for i, ref in enumerate(tile_refs):
        tiles_ref[pl.ds(i, 1)] = ref[...]
    parts_ref[...] = same_ref[...] + other_ref[...]


def owner_kernel(got_ref, *refs):
    total_ref, tiles_ref = refs[-2:]
    total = jnp.sum(got_ref[...], axis=0)
    total_ref[...] = total
    tiles_ref[...] = jnp.broadcast_to(total[None], tiles_ref.shape)


def order_of(slot, tiles):
    count = slot.shape[0]
    ids = jnp.arange(count, dtype=I32)
    names = jnp.arange(tiles, dtype=I32)
    held = jnp.sum((slot[:, None] == names[None]).astype(I32), axis=0)
    odd = held & 1
    same = (slot[None, :] == slot[:, None]) & (ids[None, :] < ids[:, None])
    before = (slot[None, :] < slot[:, None]) | same
    place = jnp.sum(before.astype(I32), axis=1) + jnp.sum(
        jnp.where(names[None] < slot[:, None], odd[None], 0), axis=1
    )
    places = jnp.arange(count + tiles, dtype=I32)
    block = (
        jnp.sum(jnp.where(place[None, :] == places[:, None], ids[None, :] + 1, 0), axis=1) - 1
    )
    ends = jnp.sum(jnp.where(names[:, None] >= names[None], (held + odd)[None], 0), axis=1)
    firsts = 2 * jnp.arange((count + tiles) // 2, dtype=I32)
    pair = jnp.sum((ends[None, :] <= firsts[:, None]).astype(I32), axis=1)
    return block, jnp.minimum(pair, tiles - 1)


def words_kernel(block_ref, cell_ref, words_ref, sorted_ref):
    per = block_ref.shape[0] // 2 // CHUNKS
    full = per // 8 * 8
    for c in range(CHUNKS):
        sorted_ref[c * LANES + full : (c + 1) * LANES, :] = jnp.zeros((LANES - full, LANES), F32)

        def move(i, carry):
            for u in range(4):
                j = i * 4 + u
                first = row(cell_ref, jnp.maximum(block_ref[2 * (c * per + j)], 0))
                second = row(cell_ref, jnp.maximum(block_ref[2 * (c * per + j) + 1], 0))
                word = columns_of(first) | (columns_of(second) << 8)
                sorted_ref[pl.ds(c * LANES + j, 1), :] = word.astype(F32)
            return carry

        lax.fori_loop(0, per // 4, move, 0)
        words_ref[c] = sorted_ref[c * LANES : (c + 1) * LANES, :].T.astype(I32)


def fold_8(values):
    sub = lax.broadcasted_iota(I32, (8, LANES), 0)
    for width in (4, 2, 1):
        keep = (sub & width) == 0
        count = len(values) // 2
        folded = []
        for i in range(count):
            a, b = values[i], values[i + count]
            kept, moved = jnp.where(keep, a, b), jnp.where(keep, b, a)
            if width == 4:
                folded.append(kept + pltpu.roll(moved, 4, 0))
            else:
                up, down = pltpu.roll(moved, 8 - width, 0), pltpu.roll(moved, width, 0)
                folded.append(kept + jnp.where(keep, up, down))
        values = folded
    return values[0]


def pick_rows(slot_ref, cell_ref, table_ref, fields, out_ref, groups):
    blocks = cell_ref.shape[0]
    sub = lax.broadcasted_iota(I32, (8, LANES), 0)

    def eight(base):
        picked = [[] for _ in range(fields)]
        for s in range(8):
            d = slot_ref[base + s]
            cell = jnp.broadcast_to(row(cell_ref, base + s), (8, LANES))
            column, top, low = cell & 127, cell >> 10, (cell >> 7) & 7
            for f in range(fields):
                acc = None
                for q in range(table_ref.shape[2] // 8):
                    got = jnp.take_along_axis(
                        table_ref[d, f, 8 * q : 8 * q + 8, :],
                        column,
                        axis=1,
                        mode="promise_in_bounds",
                    )
                    acc = got if acc is None else jnp.where(top == q, got, acc)
                picked[f].append(jnp.where(sub == low, acc, 0.0))
        for f in range(fields):
            out_ref[f, pl.ds(pl.multiple_of(base, 8), 8), :] = fold_8(picked[f])

    def step(i, carry):
        for u in range(groups):
            eight((i * groups + u) * 8)
        return carry

    lax.fori_loop(0, blocks // (8 * groups), step, 0)


def flow_kernel(slot_ref, cell_ref, *refs):
    group_refs, (_, out_ref, table_ref, sems) = refs[:-4], refs[-4:]
    size = group_refs[0].shape[0]
    wait_all(
        start_all(
            [(ref, table_ref.at[pl.ds(i * size, size)]) for i, ref in enumerate(group_refs)], sems
        )
    )
    pick_rows(slot_ref, cell_ref, table_ref, out_ref.shape[0], out_ref, 4)


def particle_kernel(
    dest_ref, block_ref, pair_ref, cell_ref, words_ref, vol_any, drag_any, vel_any, here_any,
    solid_any, tile_any,
    new_any, same_any, other_any, late_any,
    table_ref, solid_ref, vol_ref, drag_ref, vel_ref, here_ref, new_ref, push_ref, sum_ref, sems,
):
    tables = start_all([(solid_any, table_ref)], sems)
    rest = [
        (vol_any, vol_ref),
        (drag_any, drag_ref),
        (vel_any, vel_ref),
        (here_any, here_ref),
        (tile_any, late_any),
    ]
    others = [pltpu.make_async_copy(a, b, sems.at[1 + i]) for i, (a, b) in enumerate(rest)]
    for copy in others:
        copy.start()
    sum_ref[...] = jnp.zeros_like(sum_ref)
    wait_all(tables)
    pick_rows(dest_ref, cell_ref, table_ref, 1, solid_ref, 4)
    wait_all(others)
    blocks = cell_ref.shape[0]
    size = 32

    def react(i, carry):
        at = pl.ds(pl.multiple_of(i * size, size), size)
        rate = drag_ref[at, :] * (1.0 + solid_ref[0, at, :])
        weight = vol_ref[at, :] * rate
        scaled = TIME_STEP * rate
        below = 1.0 / (1.0 + scaled)
        for f in range(3):
            here = here_ref[f, at, :]
            new = (vel_ref[f, at, :] + scaled * here) * below
            new_ref[f, at, :] = new
            push_ref[f, at, :] = weight * (new - here)
        return carry

    lax.fori_loop(0, blocks // size, react, 0, unroll=2)
    leave = pltpu.make_async_copy(new_ref, new_any, sems.at[6])
    leave.start()
    lanes, rows = ramps()
    per = block_ref.shape[0] // 2 // CHUNKS
    unroll = 4

    def side(place):
        b = block_ref[place]
        at = jnp.maximum(b, 0)
        cell = jnp.where(b < 0, -1, row(cell_ref, at))
        return weighted_rows(cell, [push_ref[f, pl.ds(at, 1), :] for f in range(3)], rows)

    def step(c, carry):
        for i in range(per // unroll):
            got = []
            for u in range(unroll):
                j = i * unroll + u
                p = c * per + j
                left = jnp.concatenate([side(2 * p), side(2 * p + 1)], axis=1)
                right = jnp.concatenate(hot_columns(words_ref[c], j, lanes), axis=0)
                got.append((p, jnp.dot(left, right, preferred_element_type=F32)))
            for p, res in got:
                add_to(sum_ref, pair_ref[p], res, 3)
        return carry

    lax.fori_loop(0, CHUNKS, step, 0)
    low, high = halves(sum_ref)
    out = [
        pltpu.make_async_copy(high, other_any, sems.at[7]),
        pltpu.make_async_copy(low, same_any, sems.at[8]),
    ]
    for copy in out:
        copy.start()
    leave.wait()
    wait_all(out)


def combine(stacked, solid, source, neighbours):
    padded = jnp.pad(stacked, ((0, 0), (0, 0), (0, 0), (1, 1)))
    every = neighbours + [padded[..., 2:], padded[..., :-2]]
    voidage = stacked[0]
    flow = stacked[2:]
    spread = jnp.zeros_like(flow)
    for other in every:
        spread = spread + 0.5 * (voidage + other[0]) * (other[2:] - flow)
    slope = 0.5 * jnp.stack(
        [every[0][1] - every[1][1], every[2][1] - every[3][1], every[4][1] - every[5][1]]
    )
    return flow + TIME_STEP * ((1.0 + solid) * (VISCOSITY * spread + source) - slope)


def padded_2(value, sides, width, wrap):
    for axis, dim in sides:
        size, length = (lax.axis_size(axis), value.shape[dim])
        up = [(i, (i + 1) % size) for i in range(size if wrap else size - 1)]
        down = [(j, i) for i, j in up]
        last = lax.slice_in_dim(value, length - width, length, axis=dim)
        first = lax.slice_in_dim(value, 0, width, axis=dim)
        before = lax.ppermute(last, axis, up)
        after = lax.ppermute(first, axis, down)
        value = jnp.concatenate([before, value, after], axis=dim)
    return value


def along(stage, step):
    moves = []
    for i in range(2 * SIDE * SIDE):
        x, y, core = i // (2 * SIDE), (i // 2) % SIDE, i % 2
        if core == stage:
            y = (y + step) % SIDE
        else:
            x = (x + step) % SIDE
        moves.append((i, (x * SIDE + y) * 2 + core))
    return moves


def place_of(dest, me):
    x = (me // (2 * SIDE) - dest // (2 * SIDE)) % SIDE
    y = (me // 2 - dest // 2) % SIDE
    core = dest & 1
    first, second = jnp.where(core == 0, y, x), jnp.where(core == 0, x, y)
    return (core ^ (me & 1)) * SIDE * SIDE + second * SIDE + first


def on_device(fluid_vel, pressure, part_vel, part_vol, part_drag, cell_of, dest_of):
    size = lax.axis_size("azim")
    near = size // 2
    blocks, block_rows = part_vol.shape
    tile_azim, tile_axial, radial = pressure.shape
    tile_rows = tile_azim * tile_axial
    core = lax.axis_index("azim") % 2
    chips = [[2 * i + c for i in range(near)] for c in range(2)]
    twin = [(i, i ^ 1) for i in range(size)]
    dest = dest_of[:, 0]
    slot = ((dest & 1) ^ core) * near + (dest >> 1)
    arrays = lambda *shape: jax.ShapeDtypeStruct(shape, F32)
    dma = lambda count: pltpu.SemaphoreType.DMA((count,))

    def to_owners(parts):
        return lax.all_to_all(
            parts, "azim", split_axis=0, concat_axis=0, tiled=True, axis_index_groups=chips
        )

    one_sum = arrays(near, 1, tile_rows, radial)
    dep_same, dep_other, flow_tile = pl.pallas_call(
        deposit_kernel,
        out_shape=(one_sum, one_sum, arrays(1, 3, tile_rows, radial)),
        in_specs=[SMEM_SPEC] + [VMEM_SPEC] * 3,
        out_specs=(ANY_SPEC, ANY_SPEC, VMEM_SPEC),
        scratch_shapes=[
            pltpu.VMEM((size, 1, tile_rows, radial), F32),
            pltpu.VMEM((blocks // 256, LANES, LANES), I32),
            dma(2),
        ],
        compiler_params=PARAMS,
        cost_estimate=cost(7),
    )(slot, cell_of, part_vol, fluid_vel.reshape(1, 3, tile_rows, radial))

    steps = range(1, SIDE)
    dep_twin = lax.ppermute(dep_other, "azim", twin)
    tiles = [flow_tile] + [lax.ppermute(flow_tile, "azim", along(0, k)) for k in steps]
    dep_parts, first = pl.pallas_call(
        join_kernel,
        out_shape=(one_sum, arrays(SIDE, 3, tile_rows, radial)),
        in_specs=[VMEM_SPEC] * (2 + SIDE),
        out_specs=(VMEM_SPEC, VMEM_SPEC),
        compiler_params=PARAMS,
        cost_estimate=cost(2),
    )(dep_same, dep_twin, *tiles)
    groups = [first] + [lax.ppermute(first, "azim", along(1, k)) for k in steps]
    solid_flat, solid_tiles = pl.pallas_call(
        owner_kernel,
        out_shape=(arrays(1, tile_rows, radial), arrays(size, 1, tile_rows, radial)),
        in_specs=[VMEM_SPEC] + [ANY_SPEC] * (SIDE - 1),
        out_specs=(VMEM_SPEC, VMEM_SPEC),
        compiler_params=PARAMS,
        cost_estimate=cost(2),
    )(to_owners(dep_parts), *groups[1:])
    groups += [lax.ppermute(group, "azim", twin) for group in groups]
    solid_tiles = lax.all_to_all(solid_tiles, "azim", split_axis=0, concat_axis=0, tiled=True)

    block, pair = order_of(slot, size)
    words = pl.pallas_call(
        words_kernel,
        out_shape=jax.ShapeDtypeStruct((CHUNKS, LANES, LANES), I32),
        in_specs=[SMEM_SPEC, VMEM_SPEC],
        out_specs=VMEM_SPEC,
        scratch_shapes=[pltpu.VMEM((CHUNKS * LANES, LANES), F32)],
        compiler_params=PARAMS,
        cost_estimate=cost(2),
    )(block, cell_of)

    here = pl.pallas_call(
        flow_kernel,
        out_shape=arrays(3, blocks, block_rows),
        in_specs=[SMEM_SPEC, VMEM_SPEC] + [ANY_SPEC] * (2 * SIDE + 1),
        out_specs=VMEM_SPEC,
        scratch_shapes=[pltpu.VMEM((size, 3, tile_rows, radial), F32), dma(2 * SIDE)],
        compiler_params=PARAMS,
        cost_estimate=cost(18),
    )(place_of(dest, lax.axis_index("azim")), cell_of, *groups, solid_flat)
    three = (3, blocks, block_rows)
    three_sums = arrays(near, 3, tile_rows, radial)
    new_vel, src_same, src_other, solid_late = pl.pallas_call(
        particle_kernel,
        out_shape=(arrays(*three), three_sums, three_sums, arrays(1, tile_rows, radial)),
        in_specs=[SMEM_SPEC] * 3 + [VMEM_SPEC] * 2 + [ANY_SPEC] * 6,
        out_specs=(ANY_SPEC,) * 4,
        scratch_shapes=[
            pltpu.VMEM((size, 1, tile_rows, radial), F32),
            pltpu.VMEM((1, blocks, block_rows), F32),
            pltpu.VMEM((blocks, block_rows), F32),
            pltpu.VMEM((blocks, block_rows), F32),
            pltpu.VMEM(three, F32),
            pltpu.VMEM(three, F32),
            pltpu.VMEM(three, F32),
            pltpu.VMEM(three, F32),
            pltpu.VMEM((size, 3, tile_rows, radial), F32),
            dma(9),
        ],
        compiler_params=PARAMS,
        cost_estimate=cost(20),
    )(
        dest, block, pair, cell_of, words, part_vol, part_drag,
        jnp.transpose(part_vel, (1, 0, 2)), here, solid_tiles, solid_flat,
    )
    source_flat = jnp.sum(to_owners(src_same + lax.ppermute(src_other, "azim", twin)), axis=0)
    part_out = jnp.transpose(new_vel, (1, 0, 2))
    solid = solid_late.reshape(tile_azim, tile_axial, radial)
    source = source_flat.reshape(3, tile_azim, tile_axial, radial)
    voidage = 1.0 / (1.0 + solid)
    stacked = jnp.concatenate([voidage[None], pressure[None], fluid_vel], 0)
    cycle_fields = padded_2(stacked, (("azim", 1),), 1, True)
    axial_fields = padded_2(stacked, (("axial", 2),), 1, False)
    neighbours = [
        cycle_fields[:, 2:],
        cycle_fields[:, :-2],
        axial_fields[:, :, 2:],
        axial_fields[:, :, :-2],
    ]
    fluid_out = combine(stacked, solid, source, neighbours)
    return (fluid_out, part_out)


def solution(mesh):
    in_specs = (
        P(None, "azim", "axial", None),
        P("azim", "axial", None),
        P(("azim", "axial"), None, None),
        P(("azim", "axial"), None),
        P(("azim", "axial"), None),
        P(("azim", "axial"), None),
        P(("azim", "axial"), None),
    )
    out_specs = (P(None, "azim", "axial", None), P(("azim", "axial"), None, None))
    return jax.shard_map(
        on_device, mesh=mesh, in_specs=in_specs, out_specs=out_specs, check_vma=False
    )
```

```python
import functools

import jax
import jax.numpy as jnp
from jax import lax
from jax.experimental import pallas as pl
from jax.experimental.pallas import tpu as pltpu
from jax.sharding import PartitionSpec as P

TIME_STEP = 0.25
VISCOSITY = 0.5
BF, F32, I32, I16 = jnp.bfloat16, jnp.float32, jnp.int32, jnp.int16
LANES = 128
HALF = 32
CHUNKS = 4
SIDE = 4
SMEM_SPEC = pl.BlockSpec(memory_space=pltpu.SMEM)
VMEM_SPEC = pl.BlockSpec(memory_space=pltpu.VMEM)
ANY_SPEC = pl.BlockSpec(memory_space=pl.ANY)
PARAMS = pltpu.CompilerParams(vmem_limit_bytes=60 * 2**20)


def cost(micros):
    return pl.CostEstimate(flops=0, transcendentals=0, bytes_accessed=int(micros * 3_000_000))


def row(ref, b):
    return ref[pl.ds(b, 1), :]


def two_parts(value):
    high = value.astype(BF)
    return high, (value - high.astype(F32)).astype(BF)


def columns_of(cell):
    return (cell & 127) | ((cell >> 12) << 7)


def ramps():
    lane = lax.broadcasted_iota(I32, (LANES, LANES), 1)
    lanes = [(lane + k * LANES).astype(I16) for k in range(2)]
    rows = lax.broadcasted_iota(I32, (HALF, LANES), 0).astype(F32).astype(BF)
    return lanes, rows


def weighted_rows(cell, values, rows):
    in_half = jnp.where(cell < 0, -1, (cell >> 7) & (HALF - 1)).astype(F32).astype(BF)
    mask = rows == jnp.broadcast_to(in_half, (HALF, LANES))
    zero = jnp.zeros((), BF)
    parts = []
    for value in values:
        for part in two_parts(value):
            parts.append(jnp.where(mask, jnp.broadcast_to(part, (HALF, LANES)), zero))
    return jnp.concatenate(parts, axis=0)


def hot_columns(words, j, lanes):
    one, zero = jnp.ones((), BF), jnp.zeros((), BF)
    word = jnp.broadcast_to(words[:, j : j + 1], (LANES, LANES)).astype(I16)
    both = (word & 255, lax.shift_right_logical(word, jnp.int16(8)))
    return [
        jnp.concatenate([jnp.where(k == ids, one, zero) for k in lanes], axis=1) for ids in both
    ]


def add_to(sum_ref, d, res, fields):
    for f in range(fields):
        at = 2 * f * HALF
        both = res[at : at + HALF] + res[at + HALF : at + 2 * HALF]
        sum_ref[d, f, 0:HALF, :] += both[:, :LANES]
        sum_ref[d, f, HALF : 2 * HALF, :] += both[:, LANES:]


def start_all(pairs, sems):
    copies = [pltpu.make_async_copy(a, b, sems.at[i]) for i, (a, b) in enumerate(pairs)]
    for copy in copies:
        copy.start()
    return copies


def wait_all(copies):
    for copy in copies:
        copy.wait()


def halves(ref):
    near = ref.shape[0] // 2
    return ref.at[pl.ds(0, near)], ref.at[pl.ds(near, near)]


def deposit_kernel(
    slot_ref, cell_ref, vol_ref, same_ref, other_ref, sum_ref, words_ref, sems
):
    sum_ref[...] = jnp.zeros_like(sum_ref)
    blocks = cell_ref.shape[0]
    for g in range(blocks // 256):
        a = columns_of(cell_ref[g * 256 : g * 256 + 128, :])
        b = columns_of(cell_ref[g * 256 + 128 : g * 256 + 256, :])
        words_ref[g] = (a | (b << 8)).astype(F32).T.astype(I32)
    lanes, rows = ramps()
    unroll = 8

    def step(g, carry):
        for i in range(LANES // unroll):
            got = []
            for u in range(unroll):
                j = i * unroll + u
                hots = hot_columns(words_ref[g], j, lanes)
                for s in range(2):
                    b = g * 256 + s * 128 + j
                    left = weighted_rows(row(cell_ref, b), [row(vol_ref, b)], rows)
                    got.append((b, jnp.dot(left, hots[s], preferred_element_type=F32)))
            for b, res in got:
                add_to(sum_ref, slot_ref[b], res, 1)
        return carry

    lax.fori_loop(0, blocks // 256, step, 0)
    low, high = halves(sum_ref)
    out = [
        pltpu.make_async_copy(high, other_ref, sems.at[0]),
        pltpu.make_async_copy(low, same_ref, sems.at[1]),
    ]
    for copy in out:
        copy.start()
    wait_all(out)


def join_kernel(same_ref, other_ref, *refs):
    tile_refs, (parts_ref, tiles_ref) = refs[:-2], refs[-2:]
    for i, ref in enumerate(tile_refs):
        tiles_ref[pl.ds(i, 1)] = ref[...]
    parts_ref[...] = same_ref[...] + other_ref[...]


def owner_kernel(got_ref, *refs):
    total_ref, tiles_ref = refs[-2:]
    total = jnp.sum(got_ref[...], axis=0)
    total_ref[...] = total
    tiles_ref[...] = jnp.broadcast_to(total[None], tiles_ref.shape)


def order_of(slot, tiles):
    count = slot.shape[0]
    ids = jnp.arange(count, dtype=I32)
    names = jnp.arange(tiles, dtype=I32)
    held = jnp.sum((slot[:, None] == names[None]).astype(I32), axis=0)
    odd = held & 1
    same = (slot[None, :] == slot[:, None]) & (ids[None, :] < ids[:, None])
    before = (slot[None, :] < slot[:, None]) | same
    place = jnp.sum(before.astype(I32), axis=1) + jnp.sum(
        jnp.where(names[None] < slot[:, None], odd[None], 0), axis=1
    )
    places = jnp.arange(count + tiles, dtype=I32)
    block = (
        jnp.sum(jnp.where(place[None, :] == places[:, None], ids[None, :] + 1, 0), axis=1) - 1
    )
    ends = jnp.sum(jnp.where(names[:, None] >= names[None], (held + odd)[None], 0), axis=1)
    firsts = 2 * jnp.arange((count + tiles) // 2, dtype=I32)
    pair = jnp.sum((ends[None, :] <= firsts[:, None]).astype(I32), axis=1)
    return block, jnp.minimum(pair, tiles - 1)


def words_kernel(block_ref, cell_ref, words_ref, sorted_ref):
    per = block_ref.shape[0] // 2 // CHUNKS
    full = per // 8 * 8
    for c in range(CHUNKS):
        sorted_ref[c * LANES + full : (c + 1) * LANES, :] = jnp.zeros((LANES - full, LANES), F32)

        def move(i, carry):
            for u in range(4):
                j = i * 4 + u
                first = row(cell_ref, jnp.maximum(block_ref[2 * (c * per + j)], 0))
                second = row(cell_ref, jnp.maximum(block_ref[2 * (c * per + j) + 1], 0))
                word = columns_of(first) | (columns_of(second) << 8)
                sorted_ref[pl.ds(c * LANES + j, 1), :] = word.astype(F32)
            return carry

        lax.fori_loop(0, per // 4, move, 0)
        words_ref[c] = sorted_ref[c * LANES : (c + 1) * LANES, :].T.astype(I32)


def fold_8(values):
    sub = lax.broadcasted_iota(I32, (8, LANES), 0)
    for width in (4, 2, 1):
        keep = (sub & width) == 0
        count = len(values) // 2
        folded = []
        for i in range(count):
            a, b = values[i], values[i + count]
            kept, moved = jnp.where(keep, a, b), jnp.where(keep, b, a)
            if width == 4:
                folded.append(kept + pltpu.roll(moved, 4, 0))
            else:
                up, down = pltpu.roll(moved, 8 - width, 0), pltpu.roll(moved, width, 0)
                folded.append(kept + jnp.where(keep, up, down))
        values = folded
    return values[0]


def pick_rows(slot_ref, cell_ref, table_ref, fields, out_ref, groups):
    blocks = cell_ref.shape[0]
    sub = lax.broadcasted_iota(I32, (8, LANES), 0)

    def eight(base):
        picked = [[] for _ in range(fields)]
        for s in range(8):
            d = slot_ref[base + s]
            cell = jnp.broadcast_to(row(cell_ref, base + s), (8, LANES))
            column, top, low = cell & 127, cell >> 10, (cell >> 7) & 7
            for f in range(fields):
                acc = None
                for q in range(table_ref.shape[2] // 8):
                    got = jnp.take_along_axis(
                        table_ref[d, f, 8 * q : 8 * q + 8, :],
                        column,
                        axis=1,
                        mode="promise_in_bounds",
                    )
                    acc = got if acc is None else jnp.where(top == q, got, acc)
                picked[f].append(jnp.where(sub == low, acc, 0.0))
        for f in range(fields):
            out_ref[f, pl.ds(pl.multiple_of(base, 8), 8), :] = fold_8(picked[f])

    def step(i, carry):
        for u in range(groups):
            eight((i * groups + u) * 8)
        return carry

    lax.fori_loop(0, blocks // (8 * groups), step, 0)


def flow_kernel(slot_ref, cell_ref, *refs):
    group_refs, (_, out_ref, table_ref, sems) = refs[:-4], refs[-4:]
    size = group_refs[0].shape[0]
    wait_all(
        start_all(
            [(ref, table_ref.at[pl.ds(i * size, size)]) for i, ref in enumerate(group_refs)], sems
        )
    )
    pick_rows(slot_ref, cell_ref, table_ref, out_ref.shape[0], out_ref, 4)


def particle_kernel(
    dest_ref, block_ref, pair_ref, cell_ref, words_ref, vol_any, drag_any, vel_any, here_any,
    solid_any, tile_any,
    new_any, same_any, other_any, late_any,
    table_ref, solid_ref, vol_ref, drag_ref, vel_ref, here_ref, new_ref, push_ref, sum_ref, sems,
):
    tables = start_all([(solid_any, table_ref)], sems)
    rest = [
        (vol_any, vol_ref),
        (drag_any, drag_ref),
        (vel_any, vel_ref),
        (here_any, here_ref),
        (tile_any, late_any),
    ]
    others = [pltpu.make_async_copy(a, b, sems.at[1 + i]) for i, (a, b) in enumerate(rest)]
    for copy in others:
        copy.start()
    sum_ref[...] = jnp.zeros_like(sum_ref)
    wait_all(tables)
    pick_rows(dest_ref, cell_ref, table_ref, 1, solid_ref, 4)
    wait_all(others)
    blocks = cell_ref.shape[0]
    size = 32

    def react(i, carry):
        at = pl.ds(pl.multiple_of(i * size, size), size)
        rate = drag_ref[at, :] * (1.0 + solid_ref[0, at, :])
        weight = vol_ref[at, :] * rate
        scaled = TIME_STEP * rate
        below = 1.0 / (1.0 + scaled)
        for f in range(3):
            here = here_ref[f, at, :]
            new = (vel_ref[f, at, :] + scaled * here) * below
            new_ref[f, at, :] = new
            push_ref[f, at, :] = weight * (new - here)
        return carry

    lax.fori_loop(0, blocks // size, react, 0, unroll=2)
    leave = pltpu.make_async_copy(new_ref, new_any, sems.at[6])
    leave.start()
    lanes, rows = ramps()
    per = block_ref.shape[0] // 2 // CHUNKS
    unroll = 4

    def side(place):
        b = block_ref[place]
        at = jnp.maximum(b, 0)
        cell = jnp.where(b < 0, -1, row(cell_ref, at))
        return weighted_rows(cell, [push_ref[f, pl.ds(at, 1), :] for f in range(3)], rows)

    def step(c, carry):
        for i in range(per // unroll):
            got = []
            for u in range(unroll):
                j = i * unroll + u
                p = c * per + j
                left = jnp.concatenate([side(2 * p), side(2 * p + 1)], axis=1)
                right = jnp.concatenate(hot_columns(words_ref[c], j, lanes), axis=0)
                got.append((p, jnp.dot(left, right, preferred_element_type=F32)))
            for p, res in got:
                add_to(sum_ref, pair_ref[p], res, 3)
        return carry

    lax.fori_loop(0, CHUNKS, step, 0)
    low, high = halves(sum_ref)
    out = [
        pltpu.make_async_copy(high, other_any, sems.at[7]),
        pltpu.make_async_copy(low, same_any, sems.at[8]),
    ]
    for copy in out:
        copy.start()
    leave.wait()
    wait_all(out)


def combine(stacked, solid, source, neighbours):
    padded = jnp.pad(stacked, ((0, 0), (0, 0), (0, 0), (1, 1)))
    every = neighbours + [padded[..., 2:], padded[..., :-2]]
    voidage = stacked[0]
    flow = stacked[2:]
    spread = jnp.zeros_like(flow)
    for other in every:
        spread = spread + 0.5 * (voidage + other[0]) * (other[2:] - flow)
    slope = 0.5 * jnp.stack(
        [every[0][1] - every[1][1], every[2][1] - every[3][1], every[4][1] - every[5][1]]
    )
    return flow + TIME_STEP * ((1.0 + solid) * (VISCOSITY * spread + source) - slope)


def padded_2(value, sides, width, wrap):
    for axis, dim in sides:
        size, length = (lax.axis_size(axis), value.shape[dim])
        up = [(i, (i + 1) % size) for i in range(size if wrap else size - 1)]
        down = [(j, i) for i, j in up]
        last = lax.slice_in_dim(value, length - width, length, axis=dim)
        first = lax.slice_in_dim(value, 0, width, axis=dim)
        before = lax.ppermute(last, axis, up)
        after = lax.ppermute(first, axis, down)
        value = jnp.concatenate([before, value, after], axis=dim)
    return value


def along(stage, step):
    moves = []
    for i in range(2 * SIDE * SIDE):
        x, y, core = i // (2 * SIDE), (i // 2) % SIDE, i % 2
        if core == stage:
            y = (y + step) % SIDE
        else:
            x = (x + step) % SIDE
        moves.append((i, (x * SIDE + y) * 2 + core))
    return moves


def place_of(dest, me):
    x = (me // (2 * SIDE) - dest // (2 * SIDE)) % SIDE
    y = (me // 2 - dest // 2) % SIDE
    core = dest & 1
    first, second = jnp.where(core == 0, y, x), jnp.where(core == 0, x, y)
    return (core ^ (me & 1)) * SIDE * SIDE + second * SIDE + first


def on_device(fluid_vel, pressure, part_vel, part_vol, part_drag, cell_of, dest_of):
    size = lax.axis_size("azim")
    near = size // 2
    blocks, block_rows = part_vol.shape
    tile_azim, tile_axial, radial = pressure.shape
    tile_rows = tile_azim * tile_axial
    core = lax.axis_index("azim") % 2
    chips = [[2 * i + c for i in range(near)] for c in range(2)]
    twin = [(i, i ^ 1) for i in range(size)]
    dest = dest_of[:, 0]
    slot = ((dest & 1) ^ core) * near + (dest >> 1)
    arrays = lambda *shape: jax.ShapeDtypeStruct(shape, F32)
    dma = lambda count: pltpu.SemaphoreType.DMA((count,))

    def to_owners(parts):
        return lax.all_to_all(
            parts, "azim", split_axis=0, concat_axis=0, tiled=True, axis_index_groups=chips
        )

    one_sum = arrays(near, 1, tile_rows, radial)
    flow_tile = fluid_vel.reshape(1, 3, tile_rows, radial)
    dep_same, dep_other = pl.pallas_call(
        deposit_kernel,
        out_shape=(one_sum, one_sum),
        in_specs=[SMEM_SPEC] + [VMEM_SPEC] * 2,
        out_specs=(ANY_SPEC, ANY_SPEC),
        scratch_shapes=[
            pltpu.VMEM((size, 1, tile_rows, radial), F32),
            pltpu.VMEM((blocks // 256, LANES, LANES), I32),
            dma(2),
        ],
        compiler_params=PARAMS,
        cost_estimate=cost(7),
    )(slot, cell_of, part_vol)

    steps = range(1, SIDE)
    dep_twin = lax.ppermute(dep_other, "azim", twin)
    tiles = [flow_tile] + [lax.ppermute(flow_tile, "azim", along(0, k)) for k in steps]
    dep_parts, first = pl.pallas_call(
        join_kernel,
        out_shape=(one_sum, arrays(SIDE, 3, tile_rows, radial)),
        in_specs=[VMEM_SPEC] * (2 + SIDE),
        out_specs=(VMEM_SPEC, VMEM_SPEC),
        compiler_params=PARAMS,
        cost_estimate=cost(2),
    )(dep_same, dep_twin, *tiles)
    groups = [first] + [lax.ppermute(first, "azim", along(1, k)) for k in steps]
    block, pair = order_of(slot, size)
    words = pl.pallas_call(
        words_kernel,
        out_shape=jax.ShapeDtypeStruct((CHUNKS, LANES, LANES), I32),
        in_specs=[SMEM_SPEC, VMEM_SPEC],
        out_specs=VMEM_SPEC,
        scratch_shapes=[pltpu.VMEM((CHUNKS * LANES, LANES), F32)],
        compiler_params=PARAMS,
        cost_estimate=cost(2),
    )(block, cell_of)

    groups += [lax.ppermute(group, "azim", twin) for group in groups]
    solid_flat, solid_tiles = pl.pallas_call(
        owner_kernel,
        out_shape=(arrays(1, tile_rows, radial), arrays(size, 1, tile_rows, radial)),
        in_specs=[VMEM_SPEC] + [ANY_SPEC] * (SIDE + 2),
        out_specs=(VMEM_SPEC, VMEM_SPEC),
        compiler_params=PARAMS,
        cost_estimate=cost(2),
    )(to_owners(dep_parts), words, pair, *groups[SIDE:])
    solid_tiles = lax.all_to_all(solid_tiles, "azim", split_axis=0, concat_axis=0, tiled=True)

    here = pl.pallas_call(
        flow_kernel,
        out_shape=arrays(3, blocks, block_rows),
        in_specs=[SMEM_SPEC, VMEM_SPEC] + [ANY_SPEC] * (2 * SIDE + 1),
        out_specs=VMEM_SPEC,
        scratch_shapes=[pltpu.VMEM((size, 3, tile_rows, radial), F32), dma(2 * SIDE)],
        compiler_params=PARAMS,
        cost_estimate=cost(18),
    )(place_of(dest, lax.axis_index("azim")), cell_of, *groups, solid_flat)
    three = (3, blocks, block_rows)
    three_sums = arrays(near, 3, tile_rows, radial)
    new_vel, src_same, src_other, solid_late = pl.pallas_call(
        particle_kernel,
        out_shape=(arrays(*three), three_sums, three_sums, arrays(1, tile_rows, radial)),
        in_specs=[SMEM_SPEC] * 3 + [VMEM_SPEC] * 2 + [ANY_SPEC] * 6,
        out_specs=(ANY_SPEC,) * 4,
        scratch_shapes=[
            pltpu.VMEM((size, 1, tile_rows, radial), F32),
            pltpu.VMEM((1, blocks, block_rows), F32),
            pltpu.VMEM((blocks, block_rows), F32),
            pltpu.VMEM((blocks, block_rows), F32),
            pltpu.VMEM(three, F32),
            pltpu.VMEM(three, F32),
            pltpu.VMEM(three, F32),
            pltpu.VMEM(three, F32),
            pltpu.VMEM((size, 3, tile_rows, radial), F32),
            dma(9),
        ],
        compiler_params=PARAMS,
        cost_estimate=cost(20),
    )(
        dest, block, pair, cell_of, words, part_vol, part_drag,
        jnp.transpose(part_vel, (1, 0, 2)), here, solid_tiles, solid_flat,
    )
    source_flat = jnp.sum(to_owners(src_same + lax.ppermute(src_other, "azim", twin)), axis=0)
    part_out = jnp.transpose(new_vel, (1, 0, 2))
    solid = solid_late.reshape(tile_azim, tile_axial, radial)
    source = source_flat.reshape(3, tile_azim, tile_axial, radial)
    voidage = 1.0 / (1.0 + solid)
    stacked = jnp.concatenate([voidage[None], pressure[None], fluid_vel], 0)
    cycle_fields = padded_2(stacked, (("azim", 1),), 1, True)
    axial_fields = padded_2(stacked, (("axial", 2),), 1, False)
    neighbours = [
        cycle_fields[:, 2:],
        cycle_fields[:, :-2],
        axial_fields[:, :, 2:],
        axial_fields[:, :, :-2],
    ]
    fluid_out = combine(stacked, solid, source, neighbours)
    return (fluid_out, part_out)


def solution(mesh):
    in_specs = (
        P(None, "azim", "axial", None),
        P("azim", "axial", None),
        P(("azim", "axial"), None, None),
        P(("azim", "axial"), None),
        P(("azim", "axial"), None),
        P(("azim", "axial"), None),
        P(("azim", "axial"), None),
    )
    out_specs = (P(None, "azim", "axial", None), P(("azim", "axial"), None, None))
    return jax.shard_map(
        on_device, mesh=mesh, in_specs=in_specs, out_specs=out_specs, check_vma=False
    )
```

```python
import functools

import jax
import jax.numpy as jnp
from jax import lax
from jax.experimental import pallas as pl
from jax.experimental.pallas import tpu as pltpu
from jax.sharding import PartitionSpec as P

TIME_STEP = 0.25
VISCOSITY = 0.5
BF, F32, I32, I16 = jnp.bfloat16, jnp.float32, jnp.int32, jnp.int16
LANES = 128
HALF = 32
CHUNKS = 4
SIDE = 4
SMEM_SPEC = pl.BlockSpec(memory_space=pltpu.SMEM)
VMEM_SPEC = pl.BlockSpec(memory_space=pltpu.VMEM)
ANY_SPEC = pl.BlockSpec(memory_space=pl.ANY)
PARAMS = pltpu.CompilerParams(vmem_limit_bytes=60 * 2**20)


def cost(micros):
    return pl.CostEstimate(flops=0, transcendentals=0, bytes_accessed=int(micros * 3_000_000))


def row(ref, b):
    return ref[pl.ds(b, 1), :]


def two_parts(value):
    high = value.astype(BF)
    return high, (value - high.astype(F32)).astype(BF)


def columns_of(cell):
    return (cell & 127) | ((cell >> 12) << 7)


def ramps():
    lane = lax.broadcasted_iota(I32, (LANES, LANES), 1)
    lanes = [(lane + k * LANES).astype(I16) for k in range(2)]
    rows = lax.broadcasted_iota(I32, (HALF, LANES), 0).astype(F32).astype(BF)
    return lanes, rows


def weighted_rows(cell, values, rows):
    in_half = jnp.where(cell < 0, -1, (cell >> 7) & (HALF - 1)).astype(F32).astype(BF)
    mask = rows == jnp.broadcast_to(in_half, (HALF, LANES))
    zero = jnp.zeros((), BF)
    parts = []
    for value in values:
        for part in two_parts(value):
            parts.append(jnp.where(mask, jnp.broadcast_to(part, (HALF, LANES)), zero))
    return jnp.concatenate(parts, axis=0)


def hot_columns(words, j, lanes):
    one, zero = jnp.ones((), BF), jnp.zeros((), BF)
    word = jnp.broadcast_to(words[:, j : j + 1], (LANES, LANES)).astype(I16)
    both = (word & 255, lax.shift_right_logical(word, jnp.int16(8)))
    return [
        jnp.concatenate([jnp.where(k == ids, one, zero) for k in lanes], axis=1) for ids in both
    ]


def add_to(sum_ref, d, res, fields):
    for f in range(fields):
        at = 2 * f * HALF
        both = res[at : at + HALF] + res[at + HALF : at + 2 * HALF]
        sum_ref[d, f, 0:HALF, :] += both[:, :LANES]
        sum_ref[d, f, HALF : 2 * HALF, :] += both[:, LANES:]


def start_all(pairs, sems):
    copies = [pltpu.make_async_copy(a, b, sems.at[i]) for i, (a, b) in enumerate(pairs)]
    for copy in copies:
        copy.start()
    return copies


def wait_all(copies):
    for copy in copies:
        copy.wait()


def halves(ref):
    near = ref.shape[0] // 2
    return ref.at[pl.ds(0, near)], ref.at[pl.ds(near, near)]


def deposit_kernel(
    dest_ref, core_ref, cell_ref, vol_ref, same_ref, other_ref, sum_ref, words_ref, sems
):
    near, core = same_ref.shape[0], core_ref[0]
    sum_ref[...] = jnp.zeros_like(sum_ref)
    blocks = cell_ref.shape[0]
    for g in range(blocks // 256):
        a = columns_of(cell_ref[g * 256 : g * 256 + 128, :])
        b = columns_of(cell_ref[g * 256 + 128 : g * 256 + 256, :])
        words_ref[g] = (a | (b << 8)).astype(F32).T.astype(I32)
    lanes, rows = ramps()
    unroll = 8

    def step(g, carry):
        for i in range(LANES // unroll):
            got = []
            for u in range(unroll):
                j = i * unroll + u
                hots = hot_columns(words_ref[g], j, lanes)
                for s in range(2):
                    b = g * 256 + s * 128 + j
                    left = weighted_rows(row(cell_ref, b), [row(vol_ref, b)], rows)
                    got.append((b, jnp.dot(left, hots[s], preferred_element_type=F32)))
            for b, res in got:
                d = dest_ref[b]
                add_to(sum_ref, ((d & 1) ^ core) * near + (d >> 1), res, 1)
        return carry

    lax.fori_loop(0, blocks // 256, step, 0)
    low, high = halves(sum_ref)
    out = [
        pltpu.make_async_copy(high, other_ref, sems.at[0]),
        pltpu.make_async_copy(low, same_ref, sems.at[1]),
    ]
    for copy in out:
        copy.start()
    wait_all(out)


def join_kernel(same_ref, other_ref, *refs):
    tile_refs, (parts_ref, tiles_ref) = refs[:-2], refs[-2:]
    for i, ref in enumerate(tile_refs):
        tiles_ref[pl.ds(i, 1)] = ref[...]
    parts_ref[...] = same_ref[...] + other_ref[...]


def owner_kernel(got_ref, *refs):
    total_ref, tiles_ref = refs[-2:]
    total = jnp.sum(got_ref[...], axis=0)
    total_ref[...] = total
    tiles_ref[...] = jnp.broadcast_to(total[None], tiles_ref.shape)


def order_of(slot, tiles):
    count = slot.shape[0]
    ids = jnp.arange(count, dtype=I32)
    names = jnp.arange(tiles, dtype=I32)
    held = jnp.sum((slot[:, None] == names[None]).astype(I32), axis=0)
    odd = held & 1
    same = (slot[None, :] == slot[:, None]) & (ids[None, :] < ids[:, None])
    before = (slot[None, :] < slot[:, None]) | same
    place = jnp.sum(before.astype(I32), axis=1) + jnp.sum(
        jnp.where(names[None] < slot[:, None], odd[None], 0), axis=1
    )
    places = jnp.arange(count + tiles, dtype=I32)
    block = (
        jnp.sum(jnp.where(place[None, :] == places[:, None], ids[None, :] + 1, 0), axis=1) - 1
    )
    ends = jnp.sum(jnp.where(names[:, None] >= names[None], (held + odd)[None], 0), axis=1)
    firsts = 2 * jnp.arange((count + tiles) // 2, dtype=I32)
    pair = jnp.sum((ends[None, :] <= firsts[:, None]).astype(I32), axis=1)
    return block, jnp.minimum(pair, tiles - 1)


def words_kernel(block_ref, cell_ref, words_ref, sorted_ref):
    per = block_ref.shape[0] // 2 // CHUNKS
    full = per // 8 * 8
    for c in range(CHUNKS):
        sorted_ref[c * LANES + full : (c + 1) * LANES, :] = jnp.zeros((LANES - full, LANES), F32)

        def move(i, carry):
            for u in range(4):
                j = i * 4 + u
                first = row(cell_ref, jnp.maximum(block_ref[2 * (c * per + j)], 0))
                second = row(cell_ref, jnp.maximum(block_ref[2 * (c * per + j) + 1], 0))
                word = columns_of(first) | (columns_of(second) << 8)
                sorted_ref[pl.ds(c * LANES + j, 1), :] = word.astype(F32)
            return carry

        lax.fori_loop(0, per // 4, move, 0)
        words_ref[c] = sorted_ref[c * LANES : (c + 1) * LANES, :].T.astype(I32)


def fold_8(values):
    sub = lax.broadcasted_iota(I32, (8, LANES), 0)
    for width in (4, 2, 1):
        keep = (sub & width) == 0
        count = len(values) // 2
        folded = []
        for i in range(count):
            a, b = values[i], values[i + count]
            kept, moved = jnp.where(keep, a, b), jnp.where(keep, b, a)
            if width == 4:
                folded.append(kept + pltpu.roll(moved, 4, 0))
            else:
                up, down = pltpu.roll(moved, 8 - width, 0), pltpu.roll(moved, width, 0)
                folded.append(kept + jnp.where(keep, up, down))
        values = folded
    return values[0]


def pick_rows(place_ref, cell_ref, table_ref, pieces_ref, out_ref, by_product):
    blocks = cell_ref.shape[0]
    fields, tile_rows = table_ref.shape[1:3]
    groups = 8
    sub = lax.broadcasted_iota(I32, (8, LANES), 0)
    columns = lax.broadcasted_iota(I32, (LANES, LANES), 0).astype(I16)
    one, zero = jnp.ones((), BF), jnp.zeros((), BF)
    multiplied = [f for f in range(fields) if any(by_product(f, s) for s in range(8))]

    def prepare(d, carry):
        for i, f in enumerate(multiplied):
            high, low = two_parts(table_ref[d, f])
            pieces_ref[d, i, 0:tile_rows, :] = high
            pieces_ref[d, i, tile_rows : 2 * tile_rows, :] = low
        return carry

    lax.fori_loop(0, table_ref.shape[0], prepare, 0, unroll=8)

    def eight(base):
        picked = [[] for _ in range(fields)]
        for s in range(8):
            d = place_ref[base + s]
            cell = jnp.broadcast_to(row(cell_ref, base + s), (8, LANES))
            column, top, low = cell & 127, cell >> 10, (cell >> 7) & 7
            if any(by_product(f, s) for f in range(fields)):
                pair = jnp.concatenate([column, column], axis=0).astype(I16)
                hot = jnp.where(columns == jnp.concatenate([pair] * 8, axis=0), one, zero)
            for f in range(fields):
                acc = None
                if by_product(f, s):
                    both = jnp.dot(
                        pieces_ref[d, multiplied.index(f)], hot, preferred_element_type=F32
                    )
                for q in range(tile_rows // 8):
                    at = 8 * q
                    if by_product(f, s):
                        got = both[at : at + 8] + both[tile_rows + at : tile_rows + at + 8]
                    else:
                        got = jnp.take_along_axis(
                            table_ref[d, f, at : at + 8, :],
                            column,
                            axis=1,
                            mode="promise_in_bounds",
                        )
                    acc = got if acc is None else jnp.where(top == q, got, acc)
                picked[f].append(jnp.where(sub == low, acc, 0.0))
        for f in range(fields):
            out_ref[f, pl.ds(pl.multiple_of(base, 8), 8), :] = fold_8(picked[f])

    def step(i, carry):
        for u in range(groups):
            eight((i * groups + u) * 8)
        return carry

    lax.fori_loop(0, blocks // (8 * groups), step, 0)


def flow_kernel(slot_ref, cell_ref, *refs):
    group_refs, (_, out_ref, table_ref, pieces_ref, sems) = refs[:-5], refs[-5:]
    size = group_refs[0].shape[0]
    wait_all(
        start_all(
            [(ref, table_ref.at[pl.ds(i * size, size)]) for i, ref in enumerate(group_refs)], sems
        )
    )
    pick_rows(slot_ref, cell_ref, table_ref, pieces_ref, out_ref, lambda f, s: f > 0)


def particle_kernel(
    dest_ref, block_ref, pair_ref, cell_ref, words_ref, vol_any, drag_any, vel_any, here_any,
    solid_any, tile_any,
    new_any, same_any, other_any, late_any,
    table_ref, pieces_ref, solid_ref, vol_ref, drag_ref, vel_ref, here_ref, new_ref, push_ref, sum_ref, sems,
):
    tables = start_all([(solid_any, table_ref)], sems)
    rest = [
        (vol_any, vol_ref),
        (drag_any, drag_ref),
        (vel_any, vel_ref),
        (here_any, here_ref),
        (tile_any, late_any),
    ]
    others = [pltpu.make_async_copy(a, b, sems.at[1 + i]) for i, (a, b) in enumerate(rest)]
    for copy in others:
        copy.start()
    sum_ref[...] = jnp.zeros_like(sum_ref)
    wait_all(tables)
    pick_rows(dest_ref, cell_ref, table_ref, pieces_ref, solid_ref, lambda f, s: s % 2 == 0)
    wait_all(others)
    blocks = cell_ref.shape[0]
    size = 32

    def react(i, carry):
        at = pl.ds(pl.multiple_of(i * size, size), size)
        rate = drag_ref[at, :] * (1.0 + solid_ref[0, at, :])
        weight = vol_ref[at, :] * rate
        scaled = TIME_STEP * rate
        below = 1.0 / (1.0 + scaled)
        for f in range(3):
            here = here_ref[f, at, :]
            new = (vel_ref[f, at, :] + scaled * here) * below
            new_ref[f, at, :] = new
            push_ref[f, at, :] = weight * (new - here)
        return carry

    lax.fori_loop(0, blocks // size, react, 0, unroll=2)
    leave = pltpu.make_async_copy(new_ref, new_any, sems.at[6])
    leave.start()
    lanes, rows = ramps()
    per = block_ref.shape[0] // 2 // CHUNKS
    unroll = 4

    def side(place):
        b = block_ref[place]
        at = jnp.maximum(b, 0)
        cell = jnp.where(b < 0, -1, row(cell_ref, at))
        return weighted_rows(cell, [push_ref[f, pl.ds(at, 1), :] for f in range(3)], rows)

    def step(c, carry):
        for i in range(per // unroll):
            got = []
            for u in range(unroll):
                j = i * unroll + u
                p = c * per + j
                left = jnp.concatenate([side(2 * p), side(2 * p + 1)], axis=1)
                right = jnp.concatenate(hot_columns(words_ref[c], j, lanes), axis=0)
                got.append((p, jnp.dot(left, right, preferred_element_type=F32)))
            for p, res in got:
                add_to(sum_ref, pair_ref[p], res, 3)
        return carry

    lax.fori_loop(0, CHUNKS, step, 0)
    low, high = halves(sum_ref)
    out = [
        pltpu.make_async_copy(high, other_any, sems.at[7]),
        pltpu.make_async_copy(low, same_any, sems.at[8]),
    ]
    for copy in out:
        copy.start()
    leave.wait()
    wait_all(out)


def combine(stacked, solid, source, neighbours):
    padded = jnp.pad(stacked, ((0, 0), (0, 0), (0, 0), (1, 1)))
    every = neighbours + [padded[..., 2:], padded[..., :-2]]
    voidage = stacked[0]
    flow = stacked[2:]
    spread = jnp.zeros_like(flow)
    for other in every:
        spread = spread + 0.5 * (voidage + other[0]) * (other[2:] - flow)
    slope = 0.5 * jnp.stack(
        [every[0][1] - every[1][1], every[2][1] - every[3][1], every[4][1] - every[5][1]]
    )
    return flow + TIME_STEP * ((1.0 + solid) * (VISCOSITY * spread + source) - slope)


def padded_2(value, sides, width, wrap):
    for axis, dim in sides:
        size, length = (lax.axis_size(axis), value.shape[dim])
        up = [(i, (i + 1) % size) for i in range(size if wrap else size - 1)]
        down = [(j, i) for i, j in up]
        last = lax.slice_in_dim(value, length - width, length, axis=dim)
        first = lax.slice_in_dim(value, 0, width, axis=dim)
        before = lax.ppermute(last, axis, up)
        after = lax.ppermute(first, axis, down)
        value = jnp.concatenate([before, value, after], axis=dim)
    return value


def along(stage, step):
    moves = []
    for i in range(2 * SIDE * SIDE):
        x, y, core = i // (2 * SIDE), (i // 2) % SIDE, i % 2
        if core == stage:
            y = (y + step) % SIDE
        else:
            x = (x + step) % SIDE
        moves.append((i, (x * SIDE + y) * 2 + core))
    return moves


def place_of(dest, me):
    x = (me // (2 * SIDE) - dest // (2 * SIDE)) % SIDE
    y = (me // 2 - dest // 2) % SIDE
    core = dest & 1
    first, second = jnp.where(core == 0, y, x), jnp.where(core == 0, x, y)
    return (core ^ (me & 1)) * SIDE * SIDE + second * SIDE + first


def on_device(fluid_vel, pressure, part_vel, part_vol, part_drag, cell_of, dest_of):
    size = lax.axis_size("azim")
    near = size // 2
    blocks, block_rows = part_vol.shape
    tile_azim, tile_axial, radial = pressure.shape
    tile_rows = tile_azim * tile_axial
    core = lax.axis_index("azim") % 2
    chips = [[2 * i + c for i in range(near)] for c in range(2)]
    twin = [(i, i ^ 1) for i in range(size)]
    dest = dest_of[:, 0]
    slot = ((dest & 1) ^ core) * near + (dest >> 1)
    arrays = lambda *shape: jax.ShapeDtypeStruct(shape, F32)
    dma = lambda count: pltpu.SemaphoreType.DMA((count,))

    def to_owners(parts):
        return lax.all_to_all(
            parts, "azim", split_axis=0, concat_axis=0, tiled=True, axis_index_groups=chips
        )

    one_sum = arrays(near, 1, tile_rows, radial)
    flow_tile = fluid_vel.reshape(1, 3, tile_rows, radial)
    dep_same, dep_other = pl.pallas_call(
        deposit_kernel,
        out_shape=(one_sum, one_sum),
        in_specs=[SMEM_SPEC] * 2 + [VMEM_SPEC] * 2,
        out_specs=(ANY_SPEC, ANY_SPEC),
        scratch_shapes=[
            pltpu.VMEM((size, 1, tile_rows, radial), F32),
            pltpu.VMEM((blocks // 256, LANES, LANES), I32),
            dma(2),
        ],
        compiler_params=PARAMS,
        cost_estimate=cost(7),
    )(dest, core.reshape(1), cell_of, part_vol)

    steps = range(1, SIDE)
    dep_twin = lax.ppermute(dep_other, "azim", twin)
    tiles = [flow_tile] + [lax.ppermute(flow_tile, "azim", along(0, k)) for k in steps]
    dep_parts, first = pl.pallas_call(
        join_kernel,
        out_shape=(one_sum, arrays(SIDE, 3, tile_rows, radial)),
        in_specs=[VMEM_SPEC] * (2 + SIDE),
        out_specs=(VMEM_SPEC, VMEM_SPEC),
        compiler_params=PARAMS,
        cost_estimate=cost(2),
    )(dep_same, dep_twin, *tiles)
    groups = [first] + [lax.ppermute(first, "azim", along(1, k)) for k in steps]
    block, pair = order_of(slot, size)
    words = pl.pallas_call(
        words_kernel,
        out_shape=jax.ShapeDtypeStruct((CHUNKS, LANES, LANES), I32),
        in_specs=[SMEM_SPEC, VMEM_SPEC],
        out_specs=VMEM_SPEC,
        scratch_shapes=[pltpu.VMEM((CHUNKS * LANES, LANES), F32)],
        compiler_params=PARAMS,
        cost_estimate=cost(2),
    )(block, cell_of)

    groups += [lax.ppermute(group, "azim", twin) for group in groups]
    solid_flat, solid_tiles = pl.pallas_call(
        owner_kernel,
        out_shape=(arrays(1, tile_rows, radial), arrays(size, 1, tile_rows, radial)),
        in_specs=[VMEM_SPEC] + [ANY_SPEC] * (SIDE + 2),
        out_specs=(VMEM_SPEC, VMEM_SPEC),
        compiler_params=PARAMS,
        cost_estimate=cost(2),
    )(to_owners(dep_parts), words, pair, *groups[SIDE:])
    solid_tiles = lax.all_to_all(solid_tiles, "azim", split_axis=0, concat_axis=0, tiled=True)

    here = pl.pallas_call(
        flow_kernel,
        out_shape=arrays(3, blocks, block_rows),
        in_specs=[SMEM_SPEC, VMEM_SPEC] + [ANY_SPEC] * (2 * SIDE + 1),
        out_specs=VMEM_SPEC,
        scratch_shapes=[
            pltpu.VMEM((size, 3, tile_rows, radial), F32),
            pltpu.VMEM((size, 2, 2 * tile_rows, radial), BF),
            dma(2 * SIDE),
        ],
        compiler_params=PARAMS,
        cost_estimate=cost(18),
    )(place_of(dest, lax.axis_index("azim")), cell_of, *groups, solid_flat)
    three = (3, blocks, block_rows)
    three_sums = arrays(near, 3, tile_rows, radial)
    new_vel, src_same, src_other, solid_late = pl.pallas_call(
        particle_kernel,
        out_shape=(arrays(*three), three_sums, three_sums, arrays(1, tile_rows, radial)),
        in_specs=[SMEM_SPEC] * 3 + [VMEM_SPEC] * 2 + [ANY_SPEC] * 6,
        out_specs=(ANY_SPEC,) * 4,
        scratch_shapes=[
            pltpu.VMEM((size, 1, tile_rows, radial), F32),
            pltpu.VMEM((size, 1, 2 * tile_rows, radial), BF),
            pltpu.VMEM((1, blocks, block_rows), F32),
            pltpu.VMEM((blocks, block_rows), F32),
            pltpu.VMEM((blocks, block_rows), F32),
            pltpu.VMEM(three, F32),
            pltpu.VMEM(three, F32),
            pltpu.VMEM(three, F32),
            pltpu.VMEM(three, F32),
            pltpu.VMEM((size, 3, tile_rows, radial), F32),
            dma(9),
        ],
        compiler_params=PARAMS,
        cost_estimate=cost(20),
    )(
        dest, block, pair, cell_of, words, part_vol, part_drag,
        jnp.transpose(part_vel, (1, 0, 2)), here, solid_tiles, solid_flat,
    )
    source_flat = jnp.sum(to_owners(src_same + lax.ppermute(src_other, "azim", twin)), axis=0)
    part_out = jnp.transpose(new_vel, (1, 0, 2))
    solid = solid_late.reshape(tile_azim, tile_axial, radial)
    source = source_flat.reshape(3, tile_azim, tile_axial, radial)
    voidage = 1.0 / (1.0 + solid)
    stacked = jnp.concatenate([voidage[None], pressure[None], fluid_vel], 0)
    cycle_fields = padded_2(stacked, (("azim", 1),), 1, True)
    axial_fields = padded_2(stacked, (("axial", 2),), 1, False)
    neighbours = [
        cycle_fields[:, 2:],
        cycle_fields[:, :-2],
        axial_fields[:, :, 2:],
        axial_fields[:, :, :-2],
    ]
    fluid_out = combine(stacked, solid, source, neighbours)
    return (fluid_out, part_out)


def solution(mesh):
    in_specs = (
        P(None, "azim", "axial", None),
        P("azim", "axial", None),
        P(("azim", "axial"), None, None),
        P(("azim", "axial"), None),
        P(("azim", "axial"), None),
        P(("azim", "axial"), None),
        P(("azim", "axial"), None),
    )
    out_specs = (P(None, "azim", "axial", None), P(("azim", "axial"), None, None))
    return jax.shard_map(
        on_device, mesh=mesh, in_specs=in_specs, out_specs=out_specs, check_vma=False
    )
```

```python
import functools

import jax
import jax.numpy as jnp
from jax import lax
from jax.experimental import pallas as pl
from jax.experimental.pallas import tpu as pltpu
from jax.sharding import PartitionSpec as P

TIME_STEP = 0.25
VISCOSITY = 0.5
BF, F32, I32, I16 = jnp.bfloat16, jnp.float32, jnp.int32, jnp.int16
LANES = 128
HALF = 32
CHUNKS = 4
SIDE = 4
SMEM_SPEC = pl.BlockSpec(memory_space=pltpu.SMEM)
VMEM_SPEC = pl.BlockSpec(memory_space=pltpu.VMEM)
ANY_SPEC = pl.BlockSpec(memory_space=pl.ANY)
PARAMS = pltpu.CompilerParams(vmem_limit_bytes=60 * 2**20)


def cost(micros):
    return pl.CostEstimate(flops=0, transcendentals=0, bytes_accessed=int(micros * 3_000_000))


def row(ref, b):
    return ref[pl.ds(b, 1), :]


def two_parts(value):
    high = value.astype(BF)
    return high, (value - high.astype(F32)).astype(BF)


def columns_of(cell):
    return (cell & 127) | ((cell >> 12) << 7)


def ramps():
    lane = lax.broadcasted_iota(I32, (LANES, LANES), 1)
    lanes = [(lane + k * LANES).astype(I16) for k in range(2)]
    rows = lax.broadcasted_iota(I32, (HALF, LANES), 0).astype(F32).astype(BF)
    return lanes, rows


def weighted_rows(cell, values, rows):
    in_half = jnp.where(cell < 0, -1, (cell >> 7) & (HALF - 1)).astype(F32).astype(BF)
    mask = rows == jnp.broadcast_to(in_half, (HALF, LANES))
    zero = jnp.zeros((), BF)
    parts = []
    for value in values:
        for part in two_parts(value):
            parts.append(jnp.where(mask, jnp.broadcast_to(part, (HALF, LANES)), zero))
    return jnp.concatenate(parts, axis=0)


def hot_columns(words, j, lanes):
    one, zero = jnp.ones((), BF), jnp.zeros((), BF)
    word = jnp.broadcast_to(words[:, j : j + 1], (LANES, LANES)).astype(I16)
    both = (word & 255, lax.shift_right_logical(word, jnp.int16(8)))
    return [
        jnp.concatenate([jnp.where(k == ids, one, zero) for k in lanes], axis=1) for ids in both
    ]


def add_to(sum_ref, d, res, fields):
    for f in range(fields):
        at = 2 * f * HALF
        both = res[at : at + HALF] + res[at + HALF : at + 2 * HALF]
        sum_ref[d, f, 0:HALF, :] += both[:, :LANES]
        sum_ref[d, f, HALF : 2 * HALF, :] += both[:, LANES:]


def start_all(pairs, sems):
    copies = [pltpu.make_async_copy(a, b, sems.at[i]) for i, (a, b) in enumerate(pairs)]
    for copy in copies:
        copy.start()
    return copies


def wait_all(copies):
    for copy in copies:
        copy.wait()


def halves(ref):
    near = ref.shape[0] // 2
    return ref.at[pl.ds(0, near)], ref.at[pl.ds(near, near)]


def deposit_kernel(
    dest_ref, core_ref, cell_ref, vol_ref, same_ref, other_ref, sum_ref, words_ref, sems
):
    near, core = same_ref.shape[0], core_ref[0]
    sum_ref[...] = jnp.zeros_like(sum_ref)
    blocks = cell_ref.shape[0]
    for g in range(blocks // 256):
        a = columns_of(cell_ref[g * 256 : g * 256 + 128, :])
        b = columns_of(cell_ref[g * 256 + 128 : g * 256 + 256, :])
        words_ref[g] = (a | (b << 8)).astype(F32).T.astype(I32)
    lanes, rows = ramps()
    unroll = 8

    def step(g, carry):
        for i in range(LANES // unroll):
            got = []
            for u in range(unroll):
                j = i * unroll + u
                hots = hot_columns(words_ref[g], j, lanes)
                for s in range(2):
                    b = g * 256 + s * 128 + j
                    left = weighted_rows(row(cell_ref, b), [row(vol_ref, b)], rows)
                    got.append((b, jnp.dot(left, hots[s], preferred_element_type=F32)))
            for b, res in got:
                d = dest_ref[b]
                add_to(sum_ref, ((d & 1) ^ core) * near + (d >> 1), res, 1)
        return carry

    lax.fori_loop(0, blocks // 256, step, 0)
    low, high = halves(sum_ref)
    out = [
        pltpu.make_async_copy(high, other_ref, sems.at[0]),
        pltpu.make_async_copy(low, same_ref, sems.at[1]),
    ]
    for copy in out:
        copy.start()
    wait_all(out)


def join_kernel(same_ref, other_ref, *refs):
    tile_refs, (parts_ref, tiles_ref) = refs[:-2], refs[-2:]
    for i, ref in enumerate(tile_refs):
        tiles_ref[pl.ds(i, 1)] = ref[...]
    parts_ref[...] = same_ref[...] + other_ref[...]


def order_of(slot, tiles):
    count = slot.shape[0]
    ids = jnp.arange(count, dtype=I32)
    names = jnp.arange(tiles, dtype=I32)
    held = jnp.sum((slot[:, None] == names[None]).astype(I32), axis=0)
    odd = held & 1
    same = (slot[None, :] == slot[:, None]) & (ids[None, :] < ids[:, None])
    before = (slot[None, :] < slot[:, None]) | same
    place = jnp.sum(before.astype(I32), axis=1) + jnp.sum(
        jnp.where(names[None] < slot[:, None], odd[None], 0), axis=1
    )
    places = jnp.arange(count + tiles, dtype=I32)
    block = (
        jnp.sum(jnp.where(place[None, :] == places[:, None], ids[None, :] + 1, 0), axis=1) - 1
    )
    ends = jnp.sum(jnp.where(names[:, None] >= names[None], (held + odd)[None], 0), axis=1)
    firsts = 2 * jnp.arange((count + tiles) // 2, dtype=I32)
    pair = jnp.sum((ends[None, :] <= firsts[:, None]).astype(I32), axis=1)
    return block, jnp.minimum(pair, tiles - 1)


def words_kernel(block_ref, cell_ref, words_ref, sorted_ref):
    per = block_ref.shape[0] // 2 // CHUNKS
    full = per // 8 * 8
    for c in range(CHUNKS):
        sorted_ref[c * LANES + full : (c + 1) * LANES, :] = jnp.zeros((LANES - full, LANES), F32)

        def move(i, carry):
            for u in range(4):
                j = i * 4 + u
                first = row(cell_ref, jnp.maximum(block_ref[2 * (c * per + j)], 0))
                second = row(cell_ref, jnp.maximum(block_ref[2 * (c * per + j) + 1], 0))
                word = columns_of(first) | (columns_of(second) << 8)
                sorted_ref[pl.ds(c * LANES + j, 1), :] = word.astype(F32)
            return carry

        lax.fori_loop(0, per // 4, move, 0)
        words_ref[c] = sorted_ref[c * LANES : (c + 1) * LANES, :].T.astype(I32)


def fold_8(values):
    sub = lax.broadcasted_iota(I32, (8, LANES), 0)
    for width in (4, 2, 1):
        keep = (sub & width) == 0
        count = len(values) // 2
        folded = []
        for i in range(count):
            a, b = values[i], values[i + count]
            kept, moved = jnp.where(keep, a, b), jnp.where(keep, b, a)
            if width == 4:
                folded.append(kept + pltpu.roll(moved, 4, 0))
            else:
                up, down = pltpu.roll(moved, 8 - width, 0), pltpu.roll(moved, width, 0)
                folded.append(kept + jnp.where(keep, up, down))
        values = folded
    return values[0]


def pick_rows(place_ref, cell_ref, table_ref, pieces_ref, out_ref, by_product):
    blocks = cell_ref.shape[0]
    fields, tile_rows = table_ref.shape[1:3]
    groups = 8
    sub = lax.broadcasted_iota(I32, (8, LANES), 0)
    columns = lax.broadcasted_iota(I32, (LANES, LANES), 0).astype(I16)
    one, zero = jnp.ones((), BF), jnp.zeros((), BF)
    multiplied = [f for f in range(fields) if any(by_product(f, s) for s in range(8))]

    def prepare(d, carry):
        for i, f in enumerate(multiplied):
            high, low = two_parts(table_ref[d, f])
            pieces_ref[d, i, 0:tile_rows, :] = high
            pieces_ref[d, i, tile_rows : 2 * tile_rows, :] = low
        return carry

    lax.fori_loop(0, table_ref.shape[0], prepare, 0, unroll=8)

    def eight(base):
        picked = [[] for _ in range(fields)]
        for s in range(8):
            d = place_ref[base + s]
            cell = jnp.broadcast_to(row(cell_ref, base + s), (8, LANES))
            column, top, low = cell & 127, cell >> 10, (cell >> 7) & 7
            if any(by_product(f, s) for f in range(fields)):
                pair = jnp.concatenate([column, column], axis=0).astype(I16)
                hot = jnp.where(columns == jnp.concatenate([pair] * 8, axis=0), one, zero)
            for f in range(fields):
                acc = None
                if by_product(f, s):
                    both = jnp.dot(
                        pieces_ref[d, multiplied.index(f)], hot, preferred_element_type=F32
                    )
                for q in range(tile_rows // 8):
                    at = 8 * q
                    if by_product(f, s):
                        got = both[at : at + 8] + both[tile_rows + at : tile_rows + at + 8]
                    else:
                        got = jnp.take_along_axis(
                            table_ref[d, f, at : at + 8, :],
                            column,
                            axis=1,
                            mode="promise_in_bounds",
                        )
                    acc = got if acc is None else jnp.where(top == q, got, acc)
                picked[f].append(jnp.where(sub == low, acc, 0.0))
        for f in range(fields):
            out_ref[f, pl.ds(pl.multiple_of(base, 8), 8), :] = fold_8(picked[f])

    def step(i, carry):
        for u in range(groups):
            eight((i * groups + u) * 8)
        return carry

    lax.fori_loop(0, blocks // (8 * groups), step, 0)


def flow_kernel(slot_ref, cell_ref, *refs):
    group_refs, (_, out_ref, table_ref, pieces_ref, sems) = refs[:-5], refs[-5:]
    size = group_refs[0].shape[0]
    wait_all(
        start_all(
            [(ref, table_ref.at[pl.ds(i * size, size)]) for i, ref in enumerate(group_refs)], sems
        )
    )
    pick_rows(slot_ref, cell_ref, table_ref, pieces_ref, out_ref, lambda f, s: f > 0)


def particle_kernel(
    dest_ref, block_ref, pair_ref, cell_ref, words_ref, vol_any, drag_any, vel_any, here_any,
    solid_any, tile_any,
    new_any, same_any, other_any, late_any,
    table_ref, pieces_ref, solid_ref, vol_ref, drag_ref, vel_ref, here_ref, new_ref, push_ref, sum_ref, sems,
):
    tables = start_all([(solid_any, table_ref)], sems)
    rest = [
        (vol_any, vol_ref),
        (drag_any, drag_ref),
        (vel_any, vel_ref),
        (here_any, here_ref),
        (tile_any, late_any),
    ]
    others = [pltpu.make_async_copy(a, b, sems.at[1 + i]) for i, (a, b) in enumerate(rest)]
    for copy in others:
        copy.start()
    sum_ref[...] = jnp.zeros_like(sum_ref)
    wait_all(tables)
    pick_rows(dest_ref, cell_ref, table_ref, pieces_ref, solid_ref, lambda f, s: s % 2 == 0)
    wait_all(others)
    blocks = cell_ref.shape[0]
    size = 32

    def react(i, carry):
        at = pl.ds(pl.multiple_of(i * size, size), size)
        rate = drag_ref[at, :] * (1.0 + solid_ref[0, at, :])
        weight = vol_ref[at, :] * rate
        scaled = TIME_STEP * rate
        below = 1.0 / (1.0 + scaled)
        for f in range(3):
            here = here_ref[f, at, :]
            new = (vel_ref[f, at, :] + scaled * here) * below
            new_ref[f, at, :] = new
            push_ref[f, at, :] = weight * (new - here)
        return carry

    lax.fori_loop(0, blocks // size, react, 0, unroll=2)
    leave = pltpu.make_async_copy(new_ref, new_any, sems.at[6])
    leave.start()
    lanes, rows = ramps()
    per = block_ref.shape[0] // 2 // CHUNKS
    unroll = 4

    def side(place):
        b = block_ref[place]
        at = jnp.maximum(b, 0)
        cell = jnp.where(b < 0, -1, row(cell_ref, at))
        return weighted_rows(cell, [push_ref[f, pl.ds(at, 1), :] for f in range(3)], rows)

    def step(c, carry):
        for i in range(per // unroll):
            got = []
            for u in range(unroll):
                j = i * unroll + u
                p = c * per + j
                left = jnp.concatenate([side(2 * p), side(2 * p + 1)], axis=1)
                right = jnp.concatenate(hot_columns(words_ref[c], j, lanes), axis=0)
                got.append((p, jnp.dot(left, right, preferred_element_type=F32)))
            for p, res in got:
                add_to(sum_ref, pair_ref[p], res, 3)
        return carry

    lax.fori_loop(0, CHUNKS, step, 0)
    low, high = halves(sum_ref)
    out = [
        pltpu.make_async_copy(high, other_any, sems.at[7]),
        pltpu.make_async_copy(low, same_any, sems.at[8]),
    ]
    for copy in out:
        copy.start()
    leave.wait()
    wait_all(out)


def combine(stacked, solid, source, neighbours):
    padded = jnp.pad(stacked, ((0, 0), (0, 0), (0, 0), (1, 1)))
    every = neighbours + [padded[..., 2:], padded[..., :-2]]
    voidage = stacked[0]
    flow = stacked[2:]
    spread = jnp.zeros_like(flow)
    for other in every:
        spread = spread + 0.5 * (voidage + other[0]) * (other[2:] - flow)
    slope = 0.5 * jnp.stack(
        [every[0][1] - every[1][1], every[2][1] - every[3][1], every[4][1] - every[5][1]]
    )
    return flow + TIME_STEP * ((1.0 + solid) * (VISCOSITY * spread + source) - slope)


def padded_2(value, sides, width, wrap):
    for axis, dim in sides:
        size, length = (lax.axis_size(axis), value.shape[dim])
        up = [(i, (i + 1) % size) for i in range(size if wrap else size - 1)]
        down = [(j, i) for i, j in up]
        last = lax.slice_in_dim(value, length - width, length, axis=dim)
        first = lax.slice_in_dim(value, 0, width, axis=dim)
        before = lax.ppermute(last, axis, up)
        after = lax.ppermute(first, axis, down)
        value = jnp.concatenate([before, value, after], axis=dim)
    return value


def along(stage, step):
    moves = []
    for i in range(2 * SIDE * SIDE):
        x, y, core = i // (2 * SIDE), (i // 2) % SIDE, i % 2
        if core == stage:
            y = (y + step) % SIDE
        else:
            x = (x + step) % SIDE
        moves.append((i, (x * SIDE + y) * 2 + core))
    return moves


def place_of(dest, me):
    x = (me // (2 * SIDE) - dest // (2 * SIDE)) % SIDE
    y = (me // 2 - dest // 2) % SIDE
    core = dest & 1
    first, second = jnp.where(core == 0, y, x), jnp.where(core == 0, x, y)
    return (core ^ (me & 1)) * SIDE * SIDE + second * SIDE + first


def on_device(fluid_vel, pressure, part_vel, part_vol, part_drag, cell_of, dest_of):
    size = lax.axis_size("azim")
    near = size // 2
    blocks, block_rows = part_vol.shape
    tile_azim, tile_axial, radial = pressure.shape
    tile_rows = tile_azim * tile_axial
    core = lax.axis_index("azim") % 2
    chips = [[2 * i + c for i in range(near)] for c in range(2)]
    twin = [(i, i ^ 1) for i in range(size)]
    dest = dest_of[:, 0]
    slot = ((dest & 1) ^ core) * near + (dest >> 1)
    arrays = lambda *shape: jax.ShapeDtypeStruct(shape, F32)
    dma = lambda count: pltpu.SemaphoreType.DMA((count,))

    def to_owners(parts):
        return lax.all_to_all(
            parts, "azim", split_axis=0, concat_axis=0, tiled=True, axis_index_groups=chips
        )

    one_sum = arrays(near, 1, tile_rows, radial)
    flow_tile = fluid_vel.reshape(1, 3, tile_rows, radial)
    dep_same, dep_other = pl.pallas_call(
        deposit_kernel,
        out_shape=(one_sum, one_sum),
        in_specs=[SMEM_SPEC] * 2 + [VMEM_SPEC] * 2,
        out_specs=(ANY_SPEC, ANY_SPEC),
        scratch_shapes=[
            pltpu.VMEM((size, 1, tile_rows, radial), F32),
            pltpu.VMEM((blocks // 256, LANES, LANES), I32),
            dma(2),
        ],
        compiler_params=PARAMS,
        cost_estimate=cost(7),
    )(dest, core.reshape(1), cell_of, part_vol)

    steps = range(1, SIDE)
    dep_twin = lax.ppermute(dep_other, "azim", twin)
    tiles = [flow_tile] + [lax.ppermute(flow_tile, "azim", along(0, k)) for k in steps]
    dep_parts, first = pl.pallas_call(
        join_kernel,
        out_shape=(one_sum, arrays(SIDE, 3, tile_rows, radial)),
        in_specs=[VMEM_SPEC] * (2 + SIDE),
        out_specs=(VMEM_SPEC, VMEM_SPEC),
        compiler_params=PARAMS,
        cost_estimate=cost(2),
    )(dep_same, dep_twin, *tiles)
    groups = [first] + [lax.ppermute(first, "azim", along(1, k)) for k in steps]
    block, pair = order_of(slot, size)
    words = pl.pallas_call(
        words_kernel,
        out_shape=jax.ShapeDtypeStruct((CHUNKS, LANES, LANES), I32),
        in_specs=[SMEM_SPEC, VMEM_SPEC],
        out_specs=VMEM_SPEC,
        scratch_shapes=[pltpu.VMEM((CHUNKS * LANES, LANES), F32)],
        compiler_params=PARAMS,
        cost_estimate=cost(2),
    )(block, cell_of)

    groups += [lax.ppermute(group, "azim", twin) for group in groups]
    got, words, pair, *groups[SIDE:] = lax.optimization_barrier(
        (to_owners(dep_parts), words, pair, *groups[SIDE:])
    )
    solid_flat = jnp.sum(got, axis=0)
    solid_tiles = jnp.broadcast_to(solid_flat[None], (size,) + solid_flat.shape)
    solid_tiles = lax.all_to_all(solid_tiles, "azim", split_axis=0, concat_axis=0, tiled=True)

    here = pl.pallas_call(
        flow_kernel,
        out_shape=arrays(3, blocks, block_rows),
        in_specs=[SMEM_SPEC, VMEM_SPEC] + [ANY_SPEC] * (2 * SIDE + 1),
        out_specs=VMEM_SPEC,
        scratch_shapes=[
            pltpu.VMEM((size, 3, tile_rows, radial), F32),
            pltpu.VMEM((size, 2, 2 * tile_rows, radial), BF),
            dma(2 * SIDE),
        ],
        compiler_params=PARAMS,
        cost_estimate=cost(18),
    )(place_of(dest, lax.axis_index("azim")), cell_of, *groups, solid_flat)
    three = (3, blocks, block_rows)
    three_sums = arrays(near, 3, tile_rows, radial)
    new_vel, src_same, src_other, solid_late = pl.pallas_call(
        particle_kernel,
        out_shape=(arrays(*three), three_sums, three_sums, arrays(1, tile_rows, radial)),
        in_specs=[SMEM_SPEC] * 3 + [VMEM_SPEC] * 2 + [ANY_SPEC] * 6,
        out_specs=(ANY_SPEC,) * 4,
        scratch_shapes=[
            pltpu.VMEM((size, 1, tile_rows, radial), F32),
            pltpu.VMEM((size, 1, 2 * tile_rows, radial), BF),
            pltpu.VMEM((1, blocks, block_rows), F32),
            pltpu.VMEM((blocks, block_rows), F32),
            pltpu.VMEM((blocks, block_rows), F32),
            pltpu.VMEM(three, F32),
            pltpu.VMEM(three, F32),
            pltpu.VMEM(three, F32),
            pltpu.VMEM(three, F32),
            pltpu.VMEM((size, 3, tile_rows, radial), F32),
            dma(9),
        ],
        compiler_params=PARAMS,
        cost_estimate=cost(20),
    )(
        dest, block, pair, cell_of, words, part_vol, part_drag,
        jnp.transpose(part_vel, (1, 0, 2)), here, solid_tiles, solid_flat,
    )
    source_flat = jnp.sum(to_owners(src_same + lax.ppermute(src_other, "azim", twin)), axis=0)
    part_out = jnp.transpose(new_vel, (1, 0, 2))
    solid = solid_late.reshape(tile_azim, tile_axial, radial)
    source = source_flat.reshape(3, tile_azim, tile_axial, radial)
    voidage = 1.0 / (1.0 + solid)
    stacked = jnp.concatenate([voidage[None], pressure[None], fluid_vel], 0)
    cycle_fields = padded_2(stacked, (("azim", 1),), 1, True)
    axial_fields = padded_2(stacked, (("axial", 2),), 1, False)
    neighbours = [
        cycle_fields[:, 2:],
        cycle_fields[:, :-2],
        axial_fields[:, :, 2:],
        axial_fields[:, :, :-2],
    ]
    fluid_out = combine(stacked, solid, source, neighbours)
    return (fluid_out, part_out)


def solution(mesh):
    in_specs = (
        P(None, "azim", "axial", None),
        P("azim", "axial", None),
        P(("azim", "axial"), None, None),
        P(("azim", "axial"), None),
        P(("azim", "axial"), None),
        P(("azim", "axial"), None),
        P(("azim", "axial"), None),
    )
    out_specs = (P(None, "azim", "axial", None), P(("azim", "axial"), None, None))
    return jax.shard_map(
        on_device, mesh=mesh, in_specs=in_specs, out_specs=out_specs, check_vma=False
    )
```
